128 devices in a mesh: lat: 8 (over z, core), lon: 16 (over y, x).
Axes of the slice: x: 4, y: 4, z: 4, core: 2. Of those that a mesh axis runs over, the one named last changes fastest.
Arguments:
- grid: bfloat16 [64, 128, 4, 2560], P('lat', 'lon'), may hold values from -6 to 6
- keep_list: int32 [8, 16, 40], P('lat', 'lon'), may hold values from -1 to 63, as said below
- ln_gain: float32 [2560], replicated, may hold values from 0.25 to 1.75
- ln_bias: float32 [2560], replicated, may hold values from -2 to 2
- w_qkv: bfloat16 [16, 2560, 480], P('lon'), may hold values from -2 to 2
- w_out: bfloat16 [2560, 2560], P('lon'), may hold values from -0.125 to 0.125
Outputs:
- encoded: bfloat16 [64, 128, 4, 2560], P('lat', 'lon')
The draws below stay inside these ranges and needn't reach their ends.
Inputs may be any that keep to these rules, and one draw needn't show every extreme that they name: `keep_list`: row (a, b) lists the kept windows of that device, numbered row-major within its 8 x 8 block, in increasing order, followed by -1 in the unused slots. Every device keeps 24 to 40 windows; in every draw some device keeps 40 and some device keeps 24.
All inputs are finite; a program needn't handle non-finite values.
Results may differ from the reference program's by a relative error of at most 0.015.
The reference program's roundings to bfloat16 on the way count: a program that leaves them out, or rounds other values in their place, can miss the bound.
Values may be sent and summed in bfloat16 or wider, within the bound.
No kernel may reach another device: no remote copies, remote signals or barrier semaphores. Data moves between devices by JAX's collectives and lax.ppermute only.
A program may use at most 192 MiB of HBM per device.

```python
import jax
import jax.numpy as jnp
from jax import lax

D = 2560
HD = 160
WLAT = 8
WLON = 8
HEADS = 16
WIN_DEV = 64
MOST_KEPT_WIN = 40
FEWEST_KEPT_WIN = 24
NWLAT = 64
NWLON = 128
N_LAT = 8
N_LON = 16


def draw_keep_list(key, part):
    key = jax.random.fold_in(key, 7)
    count_random_key, pick_key, order_key = jax.random.split(key, 3)
    device_total = N_LAT * N_LON
    window_counts = jax.random.randint(count_random_key, (device_total,), FEWEST_KEPT_WIN, MOST_KEPT_WIN + 1)
    selected_devices = jax.random.permutation(pick_key, device_total)
    window_counts = window_counts.at[selected_devices[0]].set(MOST_KEPT_WIN)
    window_counts = window_counts.at[selected_devices[1]].set(FEWEST_KEPT_WIN)
    forced = jnp.arange(device_total, dtype=jnp.int32) == selected_devices[0]
    device_keys = jax.random.split(order_key, device_total)

    def draw_device(device_key, kept_count, force_last):
        window_order = jax.random.permutation(device_key, WIN_DEV)
        window_rank = jnp.argsort(window_order).astype(jnp.int32)
        last_rank = window_rank[WIN_DEV - 1]
        swapped = jnp.where(window_rank == 0, last_rank, window_rank)
        swapped = swapped.at[WIN_DEV - 1].set(0)
        window_rank = jnp.where(force_last, swapped, window_rank)
        chosen = window_rank < kept_count
        numbers = jnp.arange(WIN_DEV, dtype=jnp.int32)
        sort_score = jnp.where(chosen, numbers, WIN_DEV + numbers)
        listed = jnp.argsort(sort_score)[:MOST_KEPT_WIN].astype(jnp.int32)
        return jnp.where(jnp.arange(MOST_KEPT_WIN, dtype=jnp.int32) < kept_count, listed, -1).astype(jnp.int32)
    return jax.vmap(draw_device)(device_keys, window_counts, forced).reshape(N_LAT, N_LON, MOST_KEPT_WIN)


def draw_w_qkv(key, part):
    key = jax.random.fold_in(key, 11)
    entry_key = jax.random.fold_in(key, 0)
    shape = (HEADS, D, 3 * HD)
    columns = jnp.arange(3 * HD, dtype=jnp.int32)
    query_key_cols = columns[None, :] < 2 * HD
    entries = jnp.clip(jax.random.normal(entry_key, shape, jnp.float32), -4.0, 4.0)
    column_scale = jnp.where(query_key_cols, 1.5, 1.0)
    entries = entries * column_scale[:, None, :]
    return (entries * D ** (-0.5)).astype(jnp.bfloat16)


def level_of(key, shape, pieces, smallest, high):
    def one(dim, shards_of):
        steps = jax.random.uniform(jax.random.fold_in(jax.random.fold_in(key, 6), dim), (shards_of,), jnp.float32, smallest / len(pieces), high / len(pieces))
        return jnp.repeat(jnp.exp(steps), shape[dim] // shards_of).reshape((-1,) + (1,) * (len(shape) - dim - 1))

    gain = one(*pieces[0])
    for cut in pieces[1:]:
        gain = gain * one(*cut)
    return gain


def normal_values(key, extent, deviation, most, cuts=(), held_as=jnp.bfloat16):
    loudness = level_of(key, extent, cuts, -0.22, 0.18) if cuts else 1.0
    drawn = jax.random.normal(key, extent, jnp.float32) * deviation * loudness
    return jnp.minimum(jnp.maximum(drawn, -most), most).astype(held_as)


def setup_inputs(seed: int = 0) -> dict:
    key_list = jax.random.split(jax.random.key(seed), 7)
    return {
        "grid": normal_values(key_list[0], (NWLAT, NWLON, 4, D), 1.0, 6.0, ((0, 8), (1, 16))),
        "keep_list": draw_keep_list(jax.random.fold_in(key_list[6], 71), 0),
        "ln_gain": jnp.clip(1.0 + 0.15 * jax.random.normal(key_list[2], (D,), jnp.float32), 0.25, 1.75),
        "ln_bias": normal_values(key_list[3], (D,), 0.3, 2.0, (), jnp.float32),
        "w_qkv": draw_w_qkv(jax.random.fold_in(key_list[6], 71), 0),
        "w_out": normal_values(key_list[5], (HEADS * HD, D), (HEADS * HD) ** -0.5, 0.125, ((0, 16),)),
    }


epsilon = 1e-05

def layer_norm(tokens, ln_gain, ln_bias):
    values = tokens.astype(jnp.float32)
    center = lax.optimization_barrier(jnp.mean(values, axis=-1, keepdims=True))
    variance = lax.optimization_barrier(jnp.mean((values - center) ** 2, axis=-1, keepdims=True))
    return ((values - center) * lax.rsqrt(variance + epsilon) * ln_gain + ln_bias).astype(jnp.bfloat16)

def reference(grid, keep_list, ln_gain, ln_bias, w_qkv, w_out):
    device_total = N_LAT * N_LON
    blocks = grid.reshape(N_LAT, WLAT, N_LON, WLON, 4, D).transpose(0, 2, 1, 3, 4, 5)
    flat_blocks = blocks.reshape(device_total * WIN_DEV, 4, D)
    slot_list = keep_list.reshape(device_total, MOST_KEPT_WIN)
    usable = slot_list >= 0
    device_base = (jnp.arange(device_total, dtype=jnp.int32) * WIN_DEV)[:, None]
    flat_index = (device_base + jnp.maximum(slot_list, 0)).astype(jnp.int32).reshape(-1)
    usable = usable.reshape(-1)
    slot_total = device_total * MOST_KEPT_WIN
    kept_rows = flat_blocks[flat_index]
    normed = layer_norm(kept_rows, ln_gain, ln_bias).reshape(slot_total * 4, D)
    score_scale = 1.0 / HD ** 0.5

    def head_step(accum, head_index):
        weights_head = lax.dynamic_index_in_dim(w_qkv, head_index, 0, keepdims=False)
        projected = jnp.dot(normed, weights_head, preferred_element_type=jnp.float32).astype(jnp.bfloat16)
        projected = projected.reshape(slot_total, 4, 3 * HD)

        def position_step(position):
            picked = lax.dynamic_index_in_dim(projected, position, 1, keepdims=False)
            queries = picked[:, :HD]
            key_rows = picked[:, HD:2 * HD]
            value_rows = picked[:, 2 * HD:]
            scores = jnp.dot(queries, key_rows.T, preferred_element_type=jnp.float32) * score_scale
            masked = jnp.where(usable[None, :], scores, -1e+30)
            row_peak = lax.optimization_barrier(jnp.max(masked, axis=1))
            weights = jnp.where(usable[None, :], jnp.exp(scores - row_peak[:, None]), 0.0)
            weight_sum = lax.optimization_barrier(jnp.sum(weights, axis=1))
            weighted = jnp.dot(weights.astype(jnp.bfloat16), value_rows, preferred_element_type=jnp.float32)
            return weighted / weight_sum[:, None]
        attended = lax.map(position_step, jnp.arange(4, dtype=jnp.int32))
        attended = attended.transpose(1, 0, 2).astype(jnp.bfloat16).reshape(slot_total * 4, HD)
        out_rows = lax.dynamic_slice_in_dim(w_out, head_index * HD, HD, 0)
        partial_value = jnp.dot(attended, out_rows, preferred_element_type=jnp.float32).astype(jnp.bfloat16)
        partial_value = lax.optimization_barrier(partial_value)
        return (accum + partial_value.astype(jnp.float32), None)
    mixed, unused = lax.scan(head_step, jnp.zeros((slot_total * 4, D), jnp.float32), jnp.arange(HEADS, dtype=jnp.int32))
    result = (kept_rows.astype(jnp.float32) + mixed.reshape(slot_total, 4, D)).astype(jnp.bfloat16)
    target = jnp.where(usable, flat_index, device_total * WIN_DEV).astype(jnp.int32)
    dense = jnp.zeros((device_total * WIN_DEV, 4, D), jnp.bfloat16).at[target].set(result, mode='drop')
    dense = dense.reshape(N_LAT, N_LON, WLAT, WLON, 4, D).transpose(0, 2, 1, 3, 4, 5)
    return dense.reshape(NWLAT, NWLON, 4, D)
```

```python
import functools
import math

import jax
import jax.numpy as jnp
from jax import lax
from jax.experimental import pallas as pl
from jax.experimental.pallas import tpu as pltpu
from jax.sharding import Mesh
from jax.sharding import PartitionSpec as P

EPSILON = 1e-05
SLOTS = 40
WINDOWS = 64
D = 2560
TILES = D // 128
HD = 160
BLOCK = 4 * SLOTS
COLUMN = 4 * BLOCK
QUERIES = 320
MASKED = -1e30
UNUSED = 1024.0
VMEM_LIMIT = 60 * 1024 * 1024
BF16 = jnp.bfloat16
F32 = jnp.float32
ANY = pl.BlockSpec(memory_space=pl.ANY)
VMEM = pl.BlockSpec(memory_space=pltpu.VMEM)
SMEM = pl.BlockSpec(memory_space=pltpu.SMEM)


def ring(size, shift):
    return [(i, (i + shift) % size) for i in range(size)]


def params():
    return pltpu.CompilerParams(vmem_limit_bytes=VMEM_LIMIT)


def normed_kernel(slots, place, grid_ref, gain, bias, *refs):
    outs, tokens = refs[:4], refs[4]
    used = jnp.int32(0)
    for slot in range(SLOTS):
        window = slots[slot]
        used += (window >= 0).astype(jnp.int32)
        loaded = grid_ref[jnp.maximum(window, 0)].astype(F32)
        for tile in range(TILES):
            tokens[tile, pl.ds(4 * slot, 4), :] = loaded[:, tile * 128 : (tile + 1) * 128]
    kept = lax.broadcasted_iota(jnp.int32, (SLOTS, 1), 0) < used
    for shift in range(4):
        position = lax.rem(place[0] + shift, 4)
        values = jnp.concatenate(
            [tokens[tile, pl.ds(position, SLOTS, stride=4), :] for tile in range(TILES)], axis=1
        )
        center = jnp.mean(values, axis=1, keepdims=True)
        moved = values - center
        variance = jnp.mean(moved * moved, axis=1, keepdims=True)
        normed = moved * lax.rsqrt(variance + EPSILON) * gain[...] + bias[...]
        outs[shift][...] = jnp.where(kept, normed, UNUSED).astype(BF16)


def normed_tokens(slots, place, windows, gain, bias):
    return pl.pallas_call(
        normed_kernel,
        out_shape=[jax.ShapeDtypeStruct((SLOTS, D), BF16)] * 4,
        in_specs=[SMEM, SMEM, VMEM, VMEM, VMEM],
        out_specs=[VMEM] * 4,
        scratch_shapes=[pltpu.VMEM((TILES, 4 * SLOTS, 128), F32)],
        compiler_params=params(),
        name="normed",
    )(slots, place, windows, gain, bias)


def project_kernel(rows, place, *refs):
    count = len(rows)
    pieces, weights = refs[:count], refs[count : count + 8]
    outs = refs[count + 8 : count + 12]
    tokens, held, token_sems, weight_sems = refs[count + 12 :]
    token_copies = []
    start = 0
    for i in range(count):
        token_copies.append(
            pltpu.make_async_copy(pieces[i], tokens.at[pl.ds(start, rows[i])], token_sems.at[i])
        )
        start += rows[i]
    weight_copies = [
        pltpu.make_async_copy(weights[i], held.at[i], weight_sems.at[i]) for i in range(8)
    ]
    for copy in token_copies + weight_copies:
        copy.start()
    for copy in token_copies:
        copy.wait()
    core = place[1]
    lane = lax.broadcasted_iota(jnp.int32, (start, 128), 1)
    mask = jnp.where(tokens[:, 0:128].astype(F32)[:, 0:1] > UNUSED / 2, MASKED, 0.0)
    for head in range(4):
        for half in range(2):
            weight_copies[2 * head + half].wait()
            side = core if half == 0 else 1 - core
            result = jnp.dot(tokens[...], held[2 * head + half], preferred_element_type=F32)
            outs[head][:, pl.ds(pl.multiple_of(side * 256, 256), 256)] = result.astype(BF16)
        mixed = outs[head][:, 384:512].astype(F32)
        mixed = jnp.where(lane == 96, mask, jnp.where(lane == 97, 1.0, mixed))
        outs[head][:, 384:512] = mixed.astype(BF16)


def project(place, pieces, weights):
    rows = tuple(piece.shape[0] for piece in pieces)
    total = sum(rows)
    return pl.pallas_call(
        functools.partial(project_kernel, rows),
        out_shape=[jax.ShapeDtypeStruct((total, 512), BF16)] * 4,
        in_specs=[SMEM] + [ANY] * (len(pieces) + 8),
        out_specs=[VMEM] * 4,
        scratch_shapes=[
            pltpu.VMEM((total, D), BF16),
            pltpu.VMEM((8, D, 256), BF16),
            pltpu.SemaphoreType.DMA((len(pieces),)),
            pltpu.SemaphoreType.DMA((8,)),
        ],
        compiler_params=params(),
        cost_estimate=pl.CostEstimate(
            flops=2 * total * D * 2048, bytes_accessed=total * D * 2 + D * 4096, transcendentals=0
        ),
        name="project",
    )(place, *pieces, *weights)


def attend_kernel(place, *refs):
    sources, out, held, scores, sems = refs[:8], refs[8], refs[9], refs[10], refs[11]
    copies = [pltpu.make_async_copy(sources[i], held.at[i], sems.at[i]) for i in range(8)]
    for copy in copies:
        copy.start()
    for copy in copies:
        copy.wait()
    lane = lax.broadcasted_iota(jnp.int32, (QUERIES, 128), 1)
    scale = math.log2(math.e) / HD**0.5

    def block(index, carry):
        step, half = index // 2, lax.rem(index, 2)
        rows = pl.ds(pl.multiple_of(half * QUERIES, QUERIES), QUERIES)
        tail = pltpu.roll(held[step, rows, 384:512].astype(F32), 32, 1)
        tail = jnp.where(
            (lane >= 32) & (lane < 64), tail, jnp.where(lane == 96, 1.0, 0.0)
        ).astype(BF16)
        queries = jnp.concatenate([held[step, rows, 0:128], tail], axis=1)
        top = None
        for piece in range(8):
            keys = jnp.concatenate([held[piece, :, 128:256], held[piece, :, 384:512]], axis=1)
            score = lax.dot_general(
                queries, keys, (((1,), (1,)), ((), ())), preferred_element_type=F32
            )
            scores[:, piece * COLUMN : (piece + 1) * COLUMN] = score
            for tile in range(COLUMN // 128):
                part = score[:, tile * 128 : (tile + 1) * 128]
                top = part if top is None else jnp.maximum(top, part)
        peak = jnp.max(top, axis=1, keepdims=True)
        total = jnp.zeros((QUERIES, 256), F32)
        for piece in range(8):
            weights = jnp.exp2(
                (scores[:, piece * COLUMN : (piece + 1) * COLUMN] - peak) * scale
            ).astype(BF16)
            values = jnp.concatenate([held[piece, :, 256:384], held[piece, :, 384:512]], axis=1)
            total += jnp.dot(weights, values, preferred_element_type=F32)
        inverse = 1.0 / total[:, 225:226]
        first = total[:, 0:128] * inverse
        last = pltpu.roll(total[:, 128:256] * inverse, 64, 1)
        last = jnp.where(lane < 32, last, 0.0)
        attended = jnp.concatenate([first, last], axis=1)
        for part in range(8):
            y_shift = half * 3 if part < 4 else 1 + half
            target = (
                lax.rem(place[0] + 4 - part % 4, 4) * 16
                + lax.rem(place[2] + 4 - y_shift, 4) * 4
                + lax.rem(place[3] + 4 - step, 4)
            )
            out[target] = attended[part * SLOTS : (part + 1) * SLOTS].astype(BF16)
        return carry

    lax.fori_loop(0, 8, block, 0)


def attend(place, sources):
    return pl.pallas_call(
        attend_kernel,
        out_shape=jax.ShapeDtypeStruct((64, SLOTS, 256), BF16),
        in_specs=[SMEM] + [ANY] * 8,
        out_specs=VMEM,
        scratch_shapes=[
            pltpu.VMEM((8, COLUMN, 512), BF16),
            pltpu.VMEM((QUERIES, 8 * COLUMN), F32),
            pltpu.SemaphoreType.DMA((8,)),
        ],
        compiler_params=params(),
        cost_estimate=pl.CostEstimate(
            flops=4 * COLUMN * 8 * COLUMN * 4 * 256, bytes_accessed=8 * COLUMN * 1024, transcendentals=32 * COLUMN * COLUMN
        ),
        name="attend",
    )(place, *sources)


def finish_kernel(slots, place, grid_ref, attended, *refs):
    pieces, out = refs[:8], refs[8]
    weights, rows, mixed, sems = refs[9:]
    core = place[1]

    def copies(first):
        made = []
        for shift in range(4):
            column = pl.multiple_of(lax.rem(place[0] + 4 - shift, 4) * 640, 640)
            for side in range(2):
                made.append(
                    pltpu.make_async_copy(
                        pieces[2 * shift + side],
                        weights.at[
                            :, pl.ds(80 * (side ^ first), 80), pl.ds(column, 640)
                        ],
                        sems.at[2 * shift + side],
                    )
                )
        return made

    @pl.when(core == 0)
    def _():
        for copy in copies(0):
            copy.start()

    @pl.when(core == 1)
    def _():
        for copy in copies(1):
            copy.start()

    out[...] = jnp.zeros_like(out)
    for head in range(16):
        stacked = jnp.concatenate(
            [attended[position * 16 + head].astype(F32) for position in range(4)], axis=0
        )
        rows[head] = stacked.astype(BF16)
    for copy in copies(0):
        copy.wait()
    for tile in range(10):
        total = jnp.zeros((BLOCK, 256), F32)
        for head in range(16):
            partial = jnp.dot(
                rows[head, :, 0:HD],
                weights[head, :, tile * 256 : (tile + 1) * 256],
                preferred_element_type=F32,
            )
            total += partial.astype(BF16).astype(F32)
        mixed[2 * tile] = total[:, 0:128]
        mixed[2 * tile + 1] = total[:, 128:256]
    for slot in range(SLOTS):
        window = slots[slot]

        @pl.when(window >= 0)
        def _():
            term = jnp.concatenate(
                [mixed[tile, pl.ds(slot, 4, stride=SLOTS), :] for tile in range(TILES)], axis=1
            )
            out[window] = (grid_ref[window].astype(F32) + term).astype(BF16)


def finish(slots, place, windows, attended, pieces):
    return pl.pallas_call(
        finish_kernel,
        out_shape=jax.ShapeDtypeStruct((WINDOWS, 4, D), BF16),
        in_specs=[SMEM, SMEM, VMEM, VMEM] + [ANY] * 8,
        out_specs=VMEM,
        scratch_shapes=[
            pltpu.VMEM((16, HD, D), BF16),
            pltpu.VMEM((16, BLOCK, 256), BF16),
            pltpu.VMEM((TILES, BLOCK, 128), F32),
            pltpu.SemaphoreType.DMA((8,)),
        ],
        compiler_params=params(),
        cost_estimate=pl.CostEstimate(
            flops=2 * BLOCK * D * D, bytes_accessed=2 * D * D, transcendentals=0
        ),
        name="finish",
    )(slots, place, windows, attended, *pieces)


def shards(grid, keep_list, ln_gain, ln_bias, w_qkv, w_out):
    z, core, y, x = (lax.axis_index(name) for name in ("z", "c", "y", "x"))
    place = jnp.stack([z, core, y, x]).astype(jnp.int32)
    slots = keep_list[0, 0]
    windows = grid.reshape(WINDOWS, 4, D)

    raw = w_qkv[0]
    first = jnp.concatenate([raw[:, 0:128], raw[:, 160:288]], axis=1)
    last = jnp.concatenate(
        [raw[:, 320:448], raw[:, 128:160], raw[:, 288:320], raw[:, 448:480], jnp.zeros((D, 32), BF16)],
        axis=1,
    )
    mine = jnp.where(core == 0, first, last)
    other = jnp.where(core == 0, last, first)
    weights = [mine, other]
    for shift in (1, 2, 3):
        from_x = lax.ppermute(mine, "x", ring(4, -shift))
        weights += [from_x, lax.ppermute(from_x, "c", ring(2, 1))]

    eighth = lax.dynamic_slice(w_out, (core * 80, z * 640), (80, 640))
    quarter = lax.all_gather(eighth, ("y", "x"), axis=0)
    out_pieces = []
    for shift in range(4):
        piece = lax.ppermute(quarter, "z", ring(4, shift)) if shift else quarter
        out_pieces += [piece, lax.ppermute(piece, "c", ring(2, 1))]

    normed = normed_tokens(
        slots, place, windows, ln_gain.reshape(1, D), ln_bias.reshape(1, D)
    )
    own = jnp.concatenate(
        [normed[0]] + [lax.ppermute(normed[shift], "z", ring(4, shift)) for shift in (1, 2, 3)],
        axis=0,
    )
    below = lax.ppermute(own, "y", ring(4, 1))
    above = lax.ppermute(own, "y", ring(4, 3))
    far_top = lax.ppermute(below[: BLOCK // 2], "y", ring(4, 1))
    far_bottom = lax.ppermute(above[BLOCK // 2 :], "y", ring(4, 3))
    heads = project(place, [own, below, above, far_top, far_bottom], weights)
    local = [heads[0]] + [lax.ppermute(heads[s], "x", ring(4, s)) for s in (1, 2, 3)]
    remote = [lax.ppermute(part, "c", ring(2, 1)) for part in local]
    attended = attend(place, local + remote)
    attended = lax.all_to_all(attended, ("z", "y", "x"), 0, 0, tiled=True)
    result = finish(slots, place, windows, attended, out_pieces)
    return result.reshape(grid.shape)


def solution(mesh):
    split = Mesh(mesh.devices.reshape(4, 2, 4, 4), ("z", "c", "y", "x"))
    lat, lon = ("z", "c"), ("y", "x")
    placed = (
        P(lat, lon, None, None),
        P(lat, lon, None),
        P(),
        P(),
        P(lon, None, None),
        P(lon, None),
    )
    return jax.shard_map(
        shards, mesh=split, in_specs=placed, out_specs=P(lat, lon, None, None), check_vma=False
    )
```

```python
import functools
import math

import jax
import jax.numpy as jnp
from jax import lax
from jax.experimental import pallas as pl
from jax.experimental.pallas import tpu as pltpu
from jax.sharding import Mesh
from jax.sharding import PartitionSpec as P

EPSILON = 1e-05
SLOTS = 40
WINDOWS = 64
D = 2560
TILES = D // 128
HD = 160
BLOCK = 4 * SLOTS
COLUMN = 4 * BLOCK
QUERIES = 320
MASKED = -1e30
UNUSED = 1024.0
VMEM_LIMIT = 60 * 1024 * 1024
BF16 = jnp.bfloat16
F32 = jnp.float32
ANY = pl.BlockSpec(memory_space=pl.ANY)
VMEM = pl.BlockSpec(memory_space=pltpu.VMEM)
SMEM = pl.BlockSpec(memory_space=pltpu.SMEM)


def ring(size, shift):
    return [(i, (i + shift) % size) for i in range(size)]


def params():
    return pltpu.CompilerParams(vmem_limit_bytes=VMEM_LIMIT)


def normed_kernel(slots, place, grid_ref, gain, bias, *refs):
    outs, tokens = refs[:4], refs[4]
    used = jnp.int32(0)
    for slot in range(SLOTS):
        window = slots[slot]
        used += (window >= 0).astype(jnp.int32)
        loaded = grid_ref[jnp.maximum(window, 0)].astype(F32)
        for tile in range(TILES):
            tokens[tile, pl.ds(4 * slot, 4), :] = loaded[:, tile * 128 : (tile + 1) * 128]
    kept = lax.broadcasted_iota(jnp.int32, (SLOTS, 1), 0) < used
    for shift in range(4):
        position = lax.rem(place[0] + shift, 4)
        values = jnp.concatenate(
            [tokens[tile, pl.ds(position, SLOTS, stride=4), :] for tile in range(TILES)], axis=1
        )
        center = jnp.mean(values, axis=1, keepdims=True)
        moved = values - center
        variance = jnp.mean(moved * moved, axis=1, keepdims=True)
        normed = moved * lax.rsqrt(variance + EPSILON) * gain[...] + bias[...]
        outs[shift][...] = jnp.where(kept, normed, UNUSED).astype(BF16)


def normed_tokens(slots, place, windows, gain, bias):
    return pl.pallas_call(
        normed_kernel,
        out_shape=[jax.ShapeDtypeStruct((SLOTS, D), BF16)] * 4,
        in_specs=[SMEM, SMEM, VMEM, VMEM, VMEM],
        out_specs=[VMEM] * 4,
        scratch_shapes=[pltpu.VMEM((TILES, 4 * SLOTS, 128), F32)],
        compiler_params=params(),
        name="normed",
    )(slots, place, windows, gain, bias)


def arrange_kernel(place, raw, mine, other):
    first = jnp.concatenate([raw[0, :, 0:128], raw[0, :, 160:288]], axis=1)
    tail = jnp.concatenate(
        [
            raw[0, :, 128:160],
            raw[0, :, 288:320],
            raw[0, :, 448:480],
            jnp.zeros((raw.shape[1], 32), BF16),
        ],
        axis=1,
    )
    last = jnp.concatenate([raw[0, :, 320:448], tail], axis=1)

    @pl.when(place[1] == 0)
    def _():
        mine[...] = first
        other[...] = last

    @pl.when(place[1] == 1)
    def _():
        mine[...] = last
        other[...] = first


def arrange(place, w_qkv):
    rows = 512
    half = pl.BlockSpec((rows, 256), lambda i: (i, 0))
    return pl.pallas_call(
        arrange_kernel,
        grid=(D // rows,),
        out_shape=[jax.ShapeDtypeStruct((D, 256), BF16)] * 2,
        in_specs=[SMEM, pl.BlockSpec((1, rows, 3 * HD), lambda i: (0, i, 0))],
        out_specs=[half, half],
        compiler_params=params(),
        name="arrange",
    )(place, w_qkv)


def project_kernel(rows, layout, place, *refs):
    count, heads = len(rows), len(layout)
    parts = [(head, start, size, side) for head in range(heads) for start, size, side in layout[head]]
    pieces, weights = refs[:count], refs[count : count + len(parts)]
    outs = refs[count + len(parts) : count + len(parts) + heads]
    tokens, held, token_sems, weight_sems = refs[count + len(parts) + heads :]
    token_copies = []
    total = 0
    for i in range(count):
        token_copies.append(
            pltpu.make_async_copy(pieces[i], tokens.at[pl.ds(total, rows[i])], token_sems.at[i])
        )
        total += rows[i]
    weight_copies = []
    for i, (head, start, size, side) in enumerate(parts):
        column = pl.multiple_of((1 - place[1] if side else place[1]) * 256, 256)
        weight_copies.append(
            pltpu.make_async_copy(
                weights[i],
                held.at[head, pl.ds(start, size), pl.ds(column, 256)],
                weight_sems.at[i],
            )
        )
    for copy in token_copies + weight_copies:
        copy.start()
    for copy in token_copies:
        copy.wait()
    lane = lax.broadcasted_iota(jnp.int32, (total, 128), 1)
    mask = jnp.where(tokens[:, 0:128].astype(F32)[:, 0:1] > UNUSED / 2, MASKED, 0.0)
    for head in range(heads):
        for i in range(len(parts)):
            if parts[i][0] == head:
                weight_copies[i].wait()
        result = jnp.dot(tokens[...], held[head], preferred_element_type=F32)
        mixed = jnp.where(lane == 96, mask, jnp.where(lane == 97, 1.0, result[:, 384:512]))
        outs[head][:, 0:384] = result[:, 0:384].astype(BF16)
        outs[head][:, 384:512] = mixed.astype(BF16)


def project(place, pieces, weights):
    rows = tuple(piece.shape[0] for piece in pieces)
    layout = tuple(tuple((start, a.shape[0], side) for a, start, side in head) for head in weights)
    arrays = [a for head in weights for a, _, _ in head]
    total, heads = sum(rows), len(weights)
    return pl.pallas_call(
        functools.partial(project_kernel, rows, layout),
        out_shape=[jax.ShapeDtypeStruct((total, 512), BF16)] * heads,
        in_specs=[SMEM] + [ANY] * (len(pieces) + len(arrays)),
        out_specs=[VMEM] * heads,
        scratch_shapes=[
            pltpu.VMEM((total, D), BF16),
            pltpu.VMEM((heads, D, 512), BF16),
            pltpu.SemaphoreType.DMA((len(pieces),)),
            pltpu.SemaphoreType.DMA((len(arrays),)),
        ],
        compiler_params=params(),
        cost_estimate=pl.CostEstimate(
            flops=2 * total * D * 512 * heads,
            bytes_accessed=total * D * 2 + D * 1024 * heads,
            transcendentals=0,
        ),
        name="project",
    )(place, *pieces, *arrays)


def attend_kernel(place, *refs):
    sources, out, held, turned, scores, sems = refs[:8], *refs[8:]
    copies = [pltpu.make_async_copy(sources[i], held.at[i], sems.at[i]) for i in range(8)]
    for copy in copies:
        copy.start()
    for i in range(8):
        copies[i].wait()
        turned[i, 0:128, :] = held[i, :, 128:256].T
        turned[i, 128:256, :] = held[i, :, 384:512].T
    lane = lax.broadcasted_iota(jnp.int32, (QUERIES, 128), 1)
    scale = math.log2(math.e) / HD**0.5

    def queries_of(index):
        step, half = index // 2, lax.rem(index, 2)
        rows = pl.ds(pl.multiple_of(half * QUERIES, QUERIES), QUERIES)
        tail = pltpu.roll(held[step, rows, 384:512].astype(F32), 32, 1)
        tail = jnp.where(
            (lane >= 32) & (lane < 64), tail, jnp.where(lane == 96, 1.0, 0.0)
        ).astype(BF16)
        return jnp.concatenate([held[step, rows, 0:128], tail], axis=1)

    def score(queries, slot, piece, top):
        result = jnp.dot(queries, turned[piece], preferred_element_type=F32)
        scores[slot, :, piece * COLUMN : (piece + 1) * COLUMN] = result
        for tile in range(COLUMN // 128):
            part = result[:, tile * 128 : (tile + 1) * 128]
            top = part if top is None else jnp.maximum(top, part)
        return top

    def weigh(slot, piece, peak, total):
        weights = jnp.exp2(
            (scores[slot, :, piece * COLUMN : (piece + 1) * COLUMN] - peak) * scale
        ).astype(BF16)
        values = jnp.concatenate([held[piece, :, 256:384], held[piece, :, 384:512]], axis=1)
        result = jnp.dot(weights, values, preferred_element_type=F32)
        return result if total is None else total + result

    def emit(index, total):
        step, half = index // 2, lax.rem(index, 2)
        inverse = 1.0 / total[:, 225:226]
        first = total[:, 0:128] * inverse
        last = pltpu.roll(total[:, 128:256] * inverse, 64, 1)
        last = jnp.where(lane < 32, last, 0.0)
        attended = jnp.concatenate([first, last], axis=1)
        for part in range(8):
            y_shift = half * 3 if part < 4 else 1 + half
            target = (
                lax.rem(place[0] + 4 - part % 4, 4) * 16
                + lax.rem(place[2] + 4 - y_shift, 4) * 4
                + lax.rem(place[3] + 4 - step, 4)
            )
            out[target] = attended[part * SLOTS : (part + 1) * SLOTS].astype(BF16)

    queries, top = queries_of(jnp.int32(0)), None
    for piece in range(8):
        top = score(queries, 0, piece, top)

    def two_blocks(pair, peak):
        for slot in range(2):
            index = 2 * pair + slot
            queries, top, total = queries_of(jnp.minimum(index + 1, 7)), None, None
            for piece in range(8):
                top = score(queries, 1 - slot, piece, top)
                total = weigh(slot, piece, peak, total)
            emit(index, total)
            peak = jnp.max(top, axis=1, keepdims=True)
        return peak

    lax.fori_loop(0, 4, two_blocks, jnp.max(top, axis=1, keepdims=True))


def attend(place, sources):
    return pl.pallas_call(
        attend_kernel,
        out_shape=jax.ShapeDtypeStruct((64, SLOTS, 256), BF16),
        in_specs=[SMEM] + [ANY] * 8,
        out_specs=VMEM,
        scratch_shapes=[
            pltpu.VMEM((8, COLUMN, 512), BF16),
            pltpu.VMEM((8, 256, COLUMN), BF16),
            pltpu.VMEM((2, QUERIES, 8 * COLUMN), F32),
            pltpu.SemaphoreType.DMA((8,)),
        ],
        compiler_params=params(),
        cost_estimate=pl.CostEstimate(
            flops=4 * COLUMN * 8 * COLUMN * 4 * 256,
            bytes_accessed=8 * COLUMN * 1024,
            transcendentals=32 * COLUMN * COLUMN,
        ),
        name="attend",
    )(place, *sources)


def finish_kernel(slots, place, grid_ref, attended, mine, other, out, weights, rows, mixed, sems):
    def copies(core):
        return [
            pltpu.make_async_copy(
                (mine, other)[side].at[pl.ds(16 * plane, 16)],
                weights.at[:, pl.ds(80 * (side ^ core), 80), pl.ds(640 * plane, 640)],
                sems.at[2 * plane + side],
            )
            for plane in range(4)
            for side in range(2)
        ]

    @pl.when(place[1] == 0)
    def _():
        for copy in copies(0):
            copy.start()

    @pl.when(place[1] == 1)
    def _():
        for copy in copies(1):
            copy.start()

    out[...] = jnp.zeros_like(out)
    for head in range(16):
        stacked = jnp.concatenate(
            [attended[position * 16 + head].astype(F32) for position in range(4)], axis=0
        )
        rows[head] = stacked.astype(BF16)
    for plane in range(4):
        for copy in copies(0)[2 * plane : 2 * plane + 2]:
            copy.wait()
        for start, width in ((0, 256), (256, 256), (512, 128)):
            column = 640 * plane + start
            total = jnp.zeros((BLOCK, width), F32)
            for head in range(16):
                partial = jnp.dot(
                    rows[head, :, 0:HD],
                    weights[head, :, column : column + width],
                    preferred_element_type=F32,
                )
                total += partial.astype(BF16).astype(F32)
            for tile in range(width // 128):
                mixed[column // 128 + tile] = total[:, tile * 128 : (tile + 1) * 128]
    for slot in range(SLOTS):
        window = slots[slot]

        @pl.when(window >= 0)
        def _():
            term = jnp.concatenate(
                [mixed[tile, pl.ds(slot, 4, stride=SLOTS), :] for tile in range(TILES)], axis=1
            )
            out[window] = (grid_ref[window].astype(F32) + term).astype(BF16)


def finish(slots, place, windows, attended, mine, other):
    return pl.pallas_call(
        finish_kernel,
        out_shape=jax.ShapeDtypeStruct((WINDOWS, 4, D), BF16),
        in_specs=[SMEM, SMEM, VMEM, VMEM, ANY, ANY],
        out_specs=VMEM,
        scratch_shapes=[
            pltpu.VMEM((16, HD, D), BF16),
            pltpu.VMEM((16, BLOCK, 256), BF16),
            pltpu.VMEM((TILES, BLOCK, 128), F32),
            pltpu.SemaphoreType.DMA((8,)),
        ],
        compiler_params=params(),
        cost_estimate=pl.CostEstimate(
            flops=2 * BLOCK * D * D, bytes_accessed=2 * D * D, transcendentals=0
        ),
        name="finish",
    )(slots, place, windows, attended, mine, other)


def shards(grid, keep_list, ln_gain, ln_bias, w_qkv, w_out):
    z, core, y, x = (lax.axis_index(name) for name in ("z", "c", "y", "x"))
    place = jnp.stack([z, core, y, x]).astype(jnp.int32)
    slots = keep_list[0, 0]
    windows = grid.reshape(WINDOWS, 4, D)

    eighth = lax.dynamic_slice(w_out, (core * 80, z * 640), (80, 640))
    w_out_mine = lax.all_gather(eighth, ("z", "y", "x"), axis=0)

    mine, other = arrange(place, w_qkv)
    next_mine = lax.ppermute(mine, "x", ring(4, 3))
    last_mine = lax.ppermute(mine, "x", ring(4, 1))

    normed = normed_tokens(
        slots, place, windows, ln_gain.reshape(1, D), ln_bias.reshape(1, D)
    )
    own = jnp.concatenate(
        [normed[0]] + [lax.ppermute(normed[shift], "z", ring(4, shift)) for shift in (1, 2, 3)],
        axis=0,
    )
    below = lax.ppermute(own, "y", ring(4, 1))
    above = lax.ppermute(own, "y", ring(4, 3))

    far_first = lax.ppermute(next_mine[: D // 2], "x", ring(4, 3))
    far_last = lax.ppermute(last_mine[D // 2 :], "x", ring(4, 1))
    swap = lambda array: lax.ppermute(array, "c", ring(2, 1))
    next_other, last_other = swap(next_mine), swap(last_mine)

    far_top = lax.ppermute(below[: BLOCK // 2], "y", ring(4, 1))
    far_bottom = lax.ppermute(above[BLOCK // 2 :], "y", ring(4, 3))
    far_first_other, far_last_other = swap(far_first), swap(far_last)

    tokens = [own, below, above, far_top, far_bottom]
    to_own, to_next, to_last = project(
        place,
        tokens,
        [
            [(mine, 0, 0), (other, 0, 1)],
            [(next_mine, 0, 0), (next_other, 0, 1)],
            [(last_mine, 0, 0), (last_other, 0, 1)],
        ],
    )
    (to_far,) = project(
        place,
        tokens,
        [
            [
                (far_first, 0, 0),
                (far_last, D // 2, 0),
                (far_first_other, 0, 1),
                (far_last_other, D // 2, 1),
            ]
        ],
    )
    local = [
        to_own,
        lax.ppermute(to_next, "x", ring(4, 1)),
        lax.ppermute(to_far, "x", ring(4, 2)),
        lax.ppermute(to_last, "x", ring(4, 3)),
    ]
    remote = [swap(part) for part in local]
    attended = attend(place, local + remote)
    attended, w_out_mine = lax.optimization_barrier((attended, w_out_mine))
    w_out_other = swap(w_out_mine)
    attended = lax.all_to_all(attended, ("z", "y", "x"), 0, 0, tiled=True)
    result = finish(slots, place, windows, attended, w_out_mine, w_out_other)
    return result.reshape(grid.shape)


def solution(mesh):
    split = Mesh(mesh.devices.reshape(4, 2, 4, 4), ("z", "c", "y", "x"))
    lat, lon = ("z", "c"), ("y", "x")
    placed = (
        P(lat, lon, None, None),
        P(lat, lon, None),
        P(),
        P(),
        P(lon, None, None),
        P(lon, None),
    )
    return jax.shard_map(
        shards, mesh=split, in_specs=placed, out_specs=P(lat, lon, None, None), check_vma=False
    )
```

```python
import functools
import math

import jax
import jax.numpy as jnp
from jax import lax
from jax.experimental import pallas as pl
from jax.experimental.pallas import tpu as pltpu
from jax.sharding import Mesh
from jax.sharding import PartitionSpec as P

EPSILON = 1e-05
SLOTS = 40
WINDOWS = 64
D = 2560
TILES = D // 128
HD = 160
BLOCK = 4 * SLOTS
COLUMN = 4 * BLOCK
QUERIES = 320
MASKED = -1e30
UNUSED = 1024.0
VMEM_LIMIT = 60 * 1024 * 1024
FIRST_ROWS = ((0, 128), (160, 128))
LAST_ROWS = ((320, 128), (128, 32), (288, 32), (448, 32))
BF16 = jnp.bfloat16
F32 = jnp.float32
ANY = pl.BlockSpec(memory_space=pl.ANY)
VMEM = pl.BlockSpec(memory_space=pltpu.VMEM)
SMEM = pl.BlockSpec(memory_space=pltpu.SMEM)


def ring(size, shift):
    return [(i, (i + shift) % size) for i in range(size)]


def params():
    return pltpu.CompilerParams(vmem_limit_bytes=VMEM_LIMIT)


def normed_kernel(slots, place, grid_ref, gain_ref, bias_ref, *refs):
    gain = jnp.concatenate([gain_ref[tile : tile + 1, :] for tile in range(TILES)], axis=1)
    bias = jnp.concatenate([bias_ref[tile : tile + 1, :] for tile in range(TILES)], axis=1)
    outs, tokens = refs[:4], refs[4]
    used = jnp.int32(0)
    for slot in range(SLOTS):
        window = slots[slot]
        used += (window >= 0).astype(jnp.int32)
        loaded = grid_ref[jnp.maximum(window, 0)].astype(F32)
        for tile in range(TILES):
            tokens[tile, pl.ds(4 * slot, 4), :] = loaded[:, tile * 128 : (tile + 1) * 128]
    kept = lax.broadcasted_iota(jnp.int32, (SLOTS, 1), 0) < used
    for shift in range(4):
        position = lax.rem(place[0] + shift, 4)
        values = jnp.concatenate(
            [tokens[tile, pl.ds(position, SLOTS, stride=4), :] for tile in range(TILES)], axis=1
        )
        center = jnp.mean(values, axis=1, keepdims=True)
        moved = values - center
        variance = jnp.mean(moved * moved, axis=1, keepdims=True)
        normed = moved * lax.rsqrt(variance + EPSILON) * gain + bias
        outs[shift][...] = jnp.where(kept, normed, UNUSED).astype(BF16)


def normed_tokens(slots, place, windows, gain, bias):
    return pl.pallas_call(
        normed_kernel,
        out_shape=[jax.ShapeDtypeStruct((SLOTS, D), BF16)] * 4,
        in_specs=[SMEM, SMEM, VMEM, VMEM, VMEM],
        out_specs=[VMEM] * 4,
        scratch_shapes=[pltpu.VMEM((TILES, 4 * SLOTS, 128), F32)],
        compiler_params=params(),
        name="normed",
    )(slots, place, windows, gain, bias)


def arrange_kernel(place, raw, mine, sems):
    def copies(rows):
        made, start = [], 0
        for i, (first, size) in enumerate(rows):
            made.append(
                pltpu.make_async_copy(
                    raw.at[0, pl.ds(first, size)], mine.at[pl.ds(start, size)], sems.at[i]
                )
            )
            start += size
        return made

    @pl.when(place[1] == 0)
    def _():
        made = copies(FIRST_ROWS)
        for copy in made:
            copy.start()
        for copy in made:
            copy.wait()

    @pl.when(place[1] == 1)
    def _():
        mine[224:256, :] = jnp.zeros((32, D), BF16)
        made = copies(LAST_ROWS)
        for copy in made:
            copy.start()
        for copy in made:
            copy.wait()


def arrange(place, raw):
    return pl.pallas_call(
        arrange_kernel,
        out_shape=jax.ShapeDtypeStruct((256, D), BF16),
        in_specs=[SMEM, ANY],
        out_specs=VMEM,
        scratch_shapes=[pltpu.SemaphoreType.DMA((4,))],
        compiler_params=params(),
        name="arrange",
    )(place, raw)


def project_kernel(rows, layout, place, *refs):
    count, heads = len(rows), len(layout)
    parts = [(head, *part) for head in range(heads) for part in layout[head]]
    pieces, refs = refs[:count], refs[count:]
    weights, refs = refs[: len(parts)], refs[len(parts) :]
    outs, (tokens, held, token_sems, weight_sems) = refs[:heads], refs[heads:]
    token_copies = []
    total = 0
    for i in range(count):
        token_copies.append(
            pltpu.make_async_copy(pieces[i], tokens.at[pl.ds(total, rows[i])], token_sems.at[i])
        )
        total += rows[i]
    weight_copies = []
    for i, (head, source, target, size, side) in enumerate(parts):
        if side is not None:
            target = pl.multiple_of((1 - place[1] if side else place[1]) * 256, 256) + target
        whole = weights[i].at[0] if len(weights[i].shape) == 3 else weights[i]
        weight_copies.append(
            pltpu.make_async_copy(
                whole.at[pl.ds(source, size)], held.at[head, pl.ds(target, size)], weight_sems.at[i]
            )
        )
    for copy in token_copies + weight_copies:
        copy.start()
    for copy in token_copies:
        copy.wait()
    lane = lax.broadcasted_iota(jnp.int32, (total, 128), 1)
    mask = jnp.where(tokens[:, 0:128].astype(F32)[:, 0:1] > UNUSED / 2, MASKED, 0.0)
    for head in range(heads):
        for i in range(len(parts)):
            if parts[i][0] == head:
                weight_copies[i].wait()
        result = lax.dot_general(
            tokens[...], held[head], (((1,), (1,)), ((), ())), preferred_element_type=F32
        )
        flags = jnp.where(lane == 96, mask, jnp.where(lane == 97, 1.0, 0.0))
        outs[head][:, 0:384] = result[:, 0:384].astype(BF16)
        outs[head][:, 384:512] = jnp.where(lane < 96, result[:, 384:512], flags).astype(BF16)


def project(place, pieces, weights):
    rows = tuple(piece.shape[0] for piece in pieces)
    layout = tuple(tuple(part[1:] for part in head) for head in weights)
    arrays = [part[0] for head in weights for part in head]
    total, heads = sum(rows), len(weights)
    return pl.pallas_call(
        functools.partial(project_kernel, rows, layout),
        out_shape=[jax.ShapeDtypeStruct((total, 512), BF16)] * heads,
        in_specs=[SMEM] + [ANY] * (len(pieces) + len(arrays)),
        out_specs=[VMEM] * heads,
        scratch_shapes=[
            pltpu.VMEM((total, D), BF16),
            pltpu.VMEM((heads, 512, D), BF16),
            pltpu.SemaphoreType.DMA((len(pieces),)),
            pltpu.SemaphoreType.DMA((len(arrays),)),
        ],
        compiler_params=params(),
        cost_estimate=pl.CostEstimate(
            flops=2 * total * D * 512 * heads,
            bytes_accessed=total * D * 2 + D * 1024 * heads,
            transcendentals=0,
        ),
        name="project",
    )(place, *pieces, *arrays)


def attend_kernel(place, *refs):
    sources, out, held, turned, scores, sems = refs[:8], *refs[8:]
    copies = [pltpu.make_async_copy(sources[i], held.at[i], sems.at[i]) for i in range(8)]
    for copy in copies:
        copy.start()
    for i in range(8):
        copies[i].wait()
        turned[i, 0:128, :] = held[i, :, 128:256].T
        turned[i, 128:256, :] = held[i, :, 384:512].T
    lane = lax.broadcasted_iota(jnp.int32, (QUERIES, 128), 1)
    scale = math.log2(math.e) / HD**0.5

    def queries_of(index):
        step, half = index // 2, lax.rem(index, 2)
        rows = pl.ds(pl.multiple_of(half * QUERIES, QUERIES), QUERIES)
        tail = pltpu.roll(held[step, rows, 384:512].astype(F32), 32, 1)
        tail = jnp.where(
            (lane >= 32) & (lane < 64), tail, jnp.where(lane == 96, 1.0, 0.0)
        ).astype(BF16)
        return jnp.concatenate([held[step, rows, 0:128], tail], axis=1)

    def score(queries, slot, piece, top):
        result = jnp.dot(queries, turned[piece], preferred_element_type=F32)
        scores[slot, :, piece * COLUMN : (piece + 1) * COLUMN] = result
        for tile in range(COLUMN // 128):
            part = result[:, tile * 128 : (tile + 1) * 128]
            top = part if top is None else jnp.maximum(top, part)
        return top

    def weigh(slot, piece, peak, total):
        weights = jnp.exp2(
            (scores[slot, :, piece * COLUMN : (piece + 1) * COLUMN] - peak) * scale
        ).astype(BF16)
        values = jnp.concatenate([held[piece, :, 256:384], held[piece, :, 384:512]], axis=1)
        result = jnp.dot(weights, values, preferred_element_type=F32)
        return result if total is None else total + result

    def emit(index, total):
        step, half = index // 2, lax.rem(index, 2)
        inverse = 1.0 / total[:, 225:226]
        first = total[:, 0:128] * inverse
        last = pltpu.roll(total[:, 128:256] * inverse, 64, 1)
        last = jnp.where(lane < 32, last, 0.0)
        attended = jnp.concatenate([first, last], axis=1)
        for part in range(8):
            y_shift = half * 3 if part < 4 else 1 + half
            target = (
                lax.rem(place[0] + 4 - part % 4, 4) * 16
                + lax.rem(place[2] + 4 - y_shift, 4) * 4
                + lax.rem(place[3] + 4 - step, 4)
            )
            out[target] = attended[part * SLOTS : (part + 1) * SLOTS].astype(BF16)

    queries, top = queries_of(jnp.int32(0)), None
    for piece in range(8):
        top = score(queries, 0, piece, top)

    def two_blocks(pair, peak):
        for slot in range(2):
            index = 2 * pair + slot
            queries, top, total = queries_of(jnp.minimum(index + 1, 7)), None, None
            for piece in range(8):
                top = score(queries, 1 - slot, piece, top)
                total = weigh(slot, piece, peak, total)
            emit(index, total)
            peak = jnp.max(top, axis=1, keepdims=True)
        return peak

    lax.fori_loop(0, 4, two_blocks, jnp.max(top, axis=1, keepdims=True))


def attend(place, sources):
    return pl.pallas_call(
        attend_kernel,
        out_shape=jax.ShapeDtypeStruct((64, SLOTS, 256), BF16),
        in_specs=[SMEM] + [ANY] * 8,
        out_specs=VMEM,
        scratch_shapes=[
            pltpu.VMEM((8, COLUMN, 512), BF16),
            pltpu.VMEM((8, 256, COLUMN), BF16),
            pltpu.VMEM((2, QUERIES, 8 * COLUMN), F32),
            pltpu.SemaphoreType.DMA((8,)),
        ],
        compiler_params=params(),
        cost_estimate=pl.CostEstimate(
            flops=4 * COLUMN * 8 * COLUMN * 4 * 256,
            bytes_accessed=8 * COLUMN * 1024,
            transcendentals=32 * COLUMN * COLUMN,
        ),
        name="attend",
    )(place, *sources)


def finish_kernel(slots, place, grid_ref, attended, mine, other, out, weights, rows, mixed, sems):
    def copies(core):
        return [
            pltpu.make_async_copy(
                (mine, other)[side].at[pl.ds(16 * plane, 16)],
                weights.at[:, pl.ds(80 * (side ^ core), 80), pl.ds(640 * plane, 640)],
                sems.at[2 * plane + side],
            )
            for plane in range(4)
            for side in range(2)
        ]

    @pl.when(place[1] == 0)
    def _():
        for copy in copies(0):
            copy.start()

    @pl.when(place[1] == 1)
    def _():
        for copy in copies(1):
            copy.start()

    out[...] = jnp.zeros_like(out)
    for head in range(16):
        stacked = jnp.concatenate(
            [attended[position * 16 + head].astype(F32) for position in range(4)], axis=0
        )
        rows[head] = stacked.astype(BF16)
    for plane in range(4):
        for copy in copies(0)[2 * plane : 2 * plane + 2]:
            copy.wait()
        for start, width in ((0, 256), (256, 256), (512, 128)):
            column = 640 * plane + start
            total = jnp.zeros((BLOCK, width), F32)
            for head in range(16):
                partial = jnp.dot(
                    rows[head, :, 0:HD],
                    weights[head, :, column : column + width],
                    preferred_element_type=F32,
                )
                total += partial.astype(BF16).astype(F32)
            for tile in range(width // 128):
                mixed[column // 128 + tile] = total[:, tile * 128 : (tile + 1) * 128]
    for slot in range(SLOTS):
        window = slots[slot]

        @pl.when(window >= 0)
        def _():
            term = jnp.concatenate(
                [mixed[tile, pl.ds(slot, 4, stride=SLOTS), :] for tile in range(TILES)], axis=1
            )
            out[window] = (grid_ref[window].astype(F32) + term).astype(BF16)


def finish(slots, place, windows, attended, mine, other):
    return pl.pallas_call(
        finish_kernel,
        out_shape=jax.ShapeDtypeStruct((WINDOWS, 4, D), BF16),
        in_specs=[SMEM, SMEM, VMEM, VMEM, ANY, ANY],
        out_specs=VMEM,
        scratch_shapes=[
            pltpu.VMEM((16, HD, D), BF16),
            pltpu.VMEM((16, BLOCK, 256), BF16),
            pltpu.VMEM((TILES, BLOCK, 128), F32),
            pltpu.SemaphoreType.DMA((8,)),
        ],
        compiler_params=params(),
        cost_estimate=pl.CostEstimate(
            flops=2 * BLOCK * D * D, bytes_accessed=2 * D * D, transcendentals=0
        ),
        name="finish",
    )(slots, place, windows, attended, mine, other)


def shards(grid, keep_list, ln_gain, ln_bias, w_qkv, w_out):
    z, core, y, x = (lax.axis_index(name) for name in ("z", "c", "y", "x"))
    place = jnp.stack([z, core, y, x]).astype(jnp.int32)
    slots = keep_list[0, 0]
    windows = grid.reshape(WINDOWS, 4, D)

    raw = jnp.swapaxes(w_qkv, 1, 2)
    mine = arrange(place, raw)
    next_mine = lax.ppermute(mine, "x", ring(4, 3))
    last_mine = lax.ppermute(mine, "x", ring(4, 1))

    slots_after = lax.optimization_barrier((slots, mine))[0]
    normed = normed_tokens(
        slots_after, place, windows, ln_gain.reshape(TILES, 128), ln_bias.reshape(TILES, 128)
    )
    own = jnp.concatenate(
        [normed[0]] + [lax.ppermute(normed[shift], "z", ring(4, shift)) for shift in (1, 2, 3)],
        axis=0,
    )
    below = lax.ppermute(own, "y", ring(4, 1))
    above = lax.ppermute(own, "y", ring(4, 3))

    swap = lambda array: lax.ppermute(array, "c", ring(2, 1))
    next_mine, last_mine, _ = lax.optimization_barrier((next_mine, last_mine, own))
    far_first = lax.ppermute(next_mine[:128], "x", ring(4, 3))
    far_last = lax.ppermute(last_mine[128:], "x", ring(4, 1))
    near = jnp.concatenate([next_mine, last_mine], axis=0)
    near_other = swap(near)
    far_top = lax.ppermute(below[: BLOCK // 2], "y", ring(4, 1))
    far_bottom = lax.ppermute(above[BLOCK // 2 :], "y", ring(4, 3))

    eighth = lax.dynamic_slice(w_out, (core * 80, z * 640), (80, 640))
    eighth = lax.optimization_barrier((eighth, below, above, far_first, far_last))[0]
    w_out_mine = lax.all_gather(eighth, ("z", "y", "x"), axis=0)
    far = jnp.concatenate([far_first, far_last], axis=0)
    far_other = swap(far)

    def parts(array, other, row):
        return [(array, row, 0, 256, 0), (other, row, 0, 256, 1)]

    tokens = [own, below, above, far_top, far_bottom]
    to_next, to_last, to_far = project(
        place,
        tokens,
        [parts(near, near_other, 0), parts(near, near_other, 256), parts(far, far_other, 0)],
    )
    tokens = lax.optimization_barrier((*tokens, to_far))[:5]
    own_rows, start = [], 0
    for first, size in FIRST_ROWS + LAST_ROWS:
        own_rows.append((raw, first, start, size, None))
        start += size
    (to_own,) = project(place, tokens, [own_rows])
    local = [
        to_own,
        lax.ppermute(to_next, "x", ring(4, 1)),
        lax.ppermute(to_far, "x", ring(4, 2)),
        lax.ppermute(to_last, "x", ring(4, 3)),
    ]
    remote = [swap(part) for part in local]
    attended = attend(place, local + remote)
    w_out_mine = lax.optimization_barrier((w_out_mine, attended))[0]
    w_out_other = swap(w_out_mine)
    attended = lax.all_to_all(attended, ("z", "y", "x"), 0, 0, tiled=True)
    result = finish(slots, place, windows, attended, w_out_mine, w_out_other)
    return result.reshape(grid.shape)


def solution(mesh):
    split = Mesh(mesh.devices.reshape(4, 2, 4, 4), ("z", "c", "y", "x"))
    lat, lon = ("z", "c"), ("y", "x")
    placed = (
        P(lat, lon, None, None),
        P(lat, lon, None),
        P(),
        P(),
        P(lon, None, None),
        P(lon, None),
    )
    return jax.shard_map(
        shards, mesh=split, in_specs=placed, out_specs=P(lat, lon, None, None), check_vma=False
    )
```

```python
import functools
import math

import jax
import jax.numpy as jnp
from jax import lax
from jax.experimental import pallas as pl
from jax.experimental.pallas import tpu as pltpu
from jax.sharding import Mesh
from jax.sharding import PartitionSpec as P

EPSILON = 1e-05
SLOTS = 40
WINDOWS = 64
D = 2560
TILES = D // 128
HD = 160
BLOCK = 4 * SLOTS
COLUMN = 4 * BLOCK
QUERIES = 320
MASKED = -1e30
UNUSED = 1024.0
VMEM_LIMIT = 60 * 1024 * 1024
HALVES = ((0, 32), (64, 96), (160, 192), (224, 256), (320, 352), (384, 416), (128, 288), (448, 0))
BF16 = jnp.bfloat16
F32 = jnp.float32
ANY = pl.BlockSpec(memory_space=pl.ANY)
VMEM = pl.BlockSpec(memory_space=pltpu.VMEM)
SMEM = pl.BlockSpec(memory_space=pltpu.SMEM)


def ring(size, shift):
    return [(i, (i + shift) % size) for i in range(size)]


def params():
    return pltpu.CompilerParams(vmem_limit_bytes=VMEM_LIMIT)


def normed_kernel(slots, place, grid_ref, gain_ref, bias_ref, *refs):
    gain = jnp.concatenate([gain_ref[tile : tile + 1, :] for tile in range(TILES)], axis=1)
    bias = jnp.concatenate([bias_ref[tile : tile + 1, :] for tile in range(TILES)], axis=1)
    outs, tokens = refs[:4], refs[4]
    used = jnp.int32(0)
    for slot in range(SLOTS):
        window = slots[slot]
        used += (window >= 0).astype(jnp.int32)
        loaded = grid_ref[jnp.maximum(window, 0)].astype(F32)
        for tile in range(TILES):
            tokens[tile, pl.ds(4 * slot, 4), :] = loaded[:, tile * 128 : (tile + 1) * 128]
    kept = lax.broadcasted_iota(jnp.int32, (SLOTS, 1), 0) < used
    for shift in range(4):
        position = lax.rem(place[0] + shift, 4)
        values = jnp.concatenate(
            [tokens[tile, pl.ds(position, SLOTS, stride=4), :] for tile in range(TILES)], axis=1
        )
        center = jnp.mean(values, axis=1, keepdims=True)
        moved = values - center
        variance = jnp.mean(moved * moved, axis=1, keepdims=True)
        normed = moved * lax.rsqrt(variance + EPSILON) * gain + bias
        outs[shift][...] = jnp.where(kept, normed, UNUSED).astype(BF16)


def normed_tokens(slots, place, windows, gain, bias):
    return pl.pallas_call(
        normed_kernel,
        out_shape=[jax.ShapeDtypeStruct((SLOTS, D), BF16)] * 4,
        in_specs=[SMEM, SMEM, VMEM, VMEM, VMEM],
        out_specs=[VMEM] * 4,
        scratch_shapes=[pltpu.VMEM((TILES, 4 * SLOTS, 128), F32)],
        compiler_params=params(),
        name="normed",
    )(slots, place, windows, gain, bias)


def piece_kernel(place, raw, piece, sems):
    quarter = 4 * place[1] + place[0]
    for part in range(2):
        first = jnp.int32(HALVES[0][part])
        for i in range(1, 8):
            first = jnp.where(quarter == i, HALVES[i][part], first)
        pltpu.make_async_copy(
            raw.at[0, pl.ds(pl.multiple_of(first, 32), 32)],
            piece.at[pl.ds(32 * part, 32)],
            sems.at[part],
        ).start()
    for part in range(2):
        pltpu.make_async_copy(
            raw.at[0, pl.ds(0, 32)], piece.at[pl.ds(32 * part, 32)], sems.at[part]
        ).wait()


def quarter_of(place, raw):
    return pl.pallas_call(
        piece_kernel,
        out_shape=jax.ShapeDtypeStruct((64, D), BF16),
        in_specs=[SMEM, ANY],
        out_specs=VMEM,
        scratch_shapes=[pltpu.SemaphoreType.DMA((2,))],
        compiler_params=params(),
        name="quarter",
    )(place, raw)


def project_kernel(rows, shifts, place, *refs):
    count, heads = len(rows), len(shifts)
    pieces, weights, refs = refs[:count], refs[count], refs[count + 1 :]
    outs, (tokens, held, token_sems, weight_sems) = refs[:heads], refs[heads:]
    token_copies = []
    total = 0
    for i in range(count):
        token_copies.append(
            pltpu.make_async_copy(pieces[i], tokens.at[pl.ds(total, rows[i])], token_sems.at[i])
        )
        total += rows[i]
    weight_copies = [
        [
            pltpu.make_async_copy(
                weights.at[4 * plane + lax.rem(place[3] + shift, 4)],
                held.at[pl.ds(256 * head + 64 * plane, 64)],
                weight_sems.at[4 * head + plane],
            )
            for plane in range(4)
        ]
        for head, shift in enumerate(shifts)
    ]
    for copy in [copy for made in weight_copies for copy in made] + token_copies:
        copy.start()
    for made in weight_copies:
        for copy in made:
            copy.wait()
    lane = lax.broadcasted_iota(jnp.int32, (COLUMN, 128), 1)
    flagged = (lane >= 96) & (place[1] == 1)
    waited = 0
    for start in range(0, total, COLUMN):
        stop = start + COLUMN
        while waited < count and sum(rows[:waited]) < stop:
            token_copies[waited].wait()
            waited += 1
        chunk = tokens[start:stop]
        mask = jnp.where(chunk[:, 0:128].astype(F32)[:, 0:1] > UNUSED / 2, MASKED, 0.0)
        flags = jnp.where(lane == 96, mask, jnp.where(lane == 97, 1.0, 0.0))
        result = lax.dot_general(
            chunk, held[...], (((1,), (1,)), ((), ())), preferred_element_type=F32
        )
        for head in range(heads):
            base = 256 * head
            outs[head][start:stop, 0:128] = result[:, base : base + 128].astype(BF16)
            outs[head][start:stop, 128:256] = jnp.where(
                flagged, flags, result[:, base + 128 : base + 256]
            ).astype(BF16)


def project(place, pieces, weights, shifts):
    rows = tuple(piece.shape[0] for piece in pieces)
    total, heads = sum(rows), len(shifts)
    return pl.pallas_call(
        functools.partial(project_kernel, rows, shifts),
        out_shape=[jax.ShapeDtypeStruct((total, 256), BF16)] * heads,
        in_specs=[SMEM] + [ANY] * (len(pieces) + 1),
        out_specs=[VMEM] * heads,
        scratch_shapes=[
            pltpu.VMEM((total, D), BF16),
            pltpu.VMEM((heads * 256, D), BF16),
            pltpu.SemaphoreType.DMA((len(pieces),)),
            pltpu.SemaphoreType.DMA((4 * heads,)),
        ],
        compiler_params=params(),
        cost_estimate=pl.CostEstimate(
            flops=2 * total * D * 256 * heads,
            bytes_accessed=total * D * 2 + D * 512 * heads,
            transcendentals=0,
        ),
        name="project",
    )(place, *pieces, weights)


def attend_kernel(place, *refs):
    sources, (out, held, turned, scores, sems) = refs[:8], refs[8:]
    copies = []
    for i in range(8):
        step, foreign = i % 4, i // 4
        copies.append([])
        for side in range(2):
            base = pl.multiple_of((1 - place[1] if side else place[1]) * 256, 256)
            copies[i].append(
                pltpu.make_async_copy(
                    sources[4 * side + step].at[pl.ds(COLUMN * (foreign ^ side), COLUMN)],
                    held.at[i, :, pl.ds(base, 256)],
                    sems.at[2 * i + side],
                )
            )
    for piece in copies:
        for copy in piece:
            copy.start()
    lane = lax.broadcasted_iota(jnp.int32, (QUERIES, 128), 1)
    scale = math.log2(math.e) / HD**0.5

    def queries_of(index):
        step, half = index // 2, lax.rem(index, 2)
        rows = pl.ds(pl.multiple_of(half * QUERIES, QUERIES), QUERIES)
        tail = pltpu.roll(held[step, rows, 384:512].astype(F32), 32, 1)
        tail = jnp.where(
            (lane >= 32) & (lane < 64), tail, jnp.where(lane == 96, 1.0, 0.0)
        ).astype(BF16)
        return jnp.concatenate([held[step, rows, 0:128], tail], axis=1)

    def score(queries, slot, piece, top):
        result = jnp.dot(queries, turned[piece], preferred_element_type=F32)
        scores[slot, :, piece * COLUMN : (piece + 1) * COLUMN] = result
        for tile in range(COLUMN // 128):
            part = result[:, tile * 128 : (tile + 1) * 128]
            top = part if top is None else jnp.maximum(top, part)
        return top

    def weigh(slot, piece, peak, total):
        weights = jnp.exp2(
            (scores[slot, :, piece * COLUMN : (piece + 1) * COLUMN] - peak) * scale
        ).astype(BF16)
        values = jnp.concatenate([held[piece, :, 256:384], held[piece, :, 384:512]], axis=1)
        result = jnp.dot(weights, values, preferred_element_type=F32)
        return result if total is None else total + result

    def emit(index, total):
        step, half = index // 2, lax.rem(index, 2)
        inverse = 1.0 / total[:, 225:226]
        first = total[:, 0:128] * inverse
        last = pltpu.roll(total[:, 128:256] * inverse, 64, 1)
        last = jnp.where(lane < 32, last, 0.0)
        attended = jnp.concatenate([first, last], axis=1)
        for part in range(8):
            y_shift = half * 3 if part < 4 else 1 + half
            target = (
                lax.rem(place[0] + 4 - part % 4, 4) * 16
                + lax.rem(place[2] + 4 - y_shift, 4) * 4
                + lax.rem(place[3] + 4 - step, 4)
            )
            out[target] = attended[part * SLOTS : (part + 1) * SLOTS].astype(BF16)

    queries, top = None, None
    for piece in range(8):
        for copy in copies[piece]:
            copy.wait()
        turned[piece, 0:128, :] = held[piece, :, 128:256].T
        turned[piece, 128:256, :] = held[piece, :, 384:512].T
        queries = queries_of(jnp.int32(0)) if queries is None else queries
        top = score(queries, 0, piece, top)

    def two_blocks(pair, peak):
        for slot in range(2):
            index = 2 * pair + slot
            queries, top, total = queries_of(jnp.minimum(index + 1, 7)), None, None
            for piece in range(8):
                top = score(queries, 1 - slot, piece, top)
                total = weigh(slot, piece, peak, total)
            emit(index, total)
            peak = jnp.max(top, axis=1, keepdims=True)
        return peak

    lax.fori_loop(0, 4, two_blocks, jnp.max(top, axis=1, keepdims=True))


def attend(place, sources):
    return pl.pallas_call(
        attend_kernel,
        out_shape=jax.ShapeDtypeStruct((64, SLOTS, 256), BF16),
        in_specs=[SMEM] + [ANY] * 8,
        out_specs=VMEM,
        scratch_shapes=[
            pltpu.VMEM((8, COLUMN, 512), BF16),
            pltpu.VMEM((8, 256, COLUMN), BF16),
            pltpu.VMEM((2, QUERIES, 8 * COLUMN), F32),
            pltpu.SemaphoreType.DMA((16,)),
        ],
        compiler_params=params(),
        cost_estimate=pl.CostEstimate(
            flops=4 * COLUMN * 8 * COLUMN * 4 * 256,
            bytes_accessed=8 * COLUMN * 1024,
            transcendentals=32 * COLUMN * COLUMN,
        ),
        name="attend",
    )(place, *sources)


def finish_kernel(slots, place, grid_ref, attended, mine, other, out, weights, rows, mixed, sems):
    def copies(core):
        return [
            pltpu.make_async_copy(
                (mine, other)[side].at[pl.ds(4 * plane, 4), shift],
                weights.at[
                    :,
                    lax.rem(place[3] + 4 - shift, 4),
                    pl.ds(80 * (side ^ core), 80),
                    pl.ds(640 * plane, 640),
                ],
                sems.at[8 * plane + 4 * side + shift],
            )
            for plane in range(4)
            for side in range(2)
            for shift in range(4)
        ]

    @pl.when(place[1] == 0)
    def _():
        for copy in copies(0):
            copy.start()

    @pl.when(place[1] == 1)
    def _():
        for copy in copies(1):
            copy.start()

    out[...] = jnp.zeros_like(out)
    for head in range(16):
        stacked = jnp.concatenate(
            [attended[position * 16 + head].astype(F32) for position in range(4)], axis=0
        )
        rows[head] = stacked.astype(BF16)
    for plane in range(4):
        for copy in copies(0)[8 * plane : 8 * plane + 8]:
            copy.wait()
        for start, width in ((0, 256), (256, 256), (512, 128)):
            column = 640 * plane + start
            total = jnp.zeros((BLOCK, width), F32)
            for head in range(16):
                partial = jnp.dot(
                    rows[head, :, 0:HD],
                    weights[head // 4, head % 4, :, column : column + width],
                    preferred_element_type=F32,
                )
                total += partial.astype(BF16).astype(F32)
            for tile in range(width // 128):
                mixed[column // 128 + tile] = total[:, tile * 128 : (tile + 1) * 128]
    for slot in range(SLOTS):
        window = slots[slot]

        @pl.when(window >= 0)
        def _():
            term = jnp.concatenate(
                [mixed[tile, pl.ds(slot, 4, stride=SLOTS), :] for tile in range(TILES)], axis=1
            )
            out[window] = (grid_ref[window].astype(F32) + term).astype(BF16)


def finish(slots, place, windows, attended, mine, other):
    return pl.pallas_call(
        finish_kernel,
        out_shape=jax.ShapeDtypeStruct((WINDOWS, 4, D), BF16),
        in_specs=[SMEM, SMEM, VMEM, VMEM, ANY, ANY],
        out_specs=VMEM,
        scratch_shapes=[
            pltpu.VMEM((4, 4, HD, D), BF16),
            pltpu.VMEM((16, BLOCK, 256), BF16),
            pltpu.VMEM((TILES, BLOCK, 128), F32),
            pltpu.SemaphoreType.DMA((32,)),
        ],
        compiler_params=params(),
        cost_estimate=pl.CostEstimate(
            flops=2 * BLOCK * D * D, bytes_accessed=2 * D * D, transcendentals=0
        ),
        name="finish",
    )(slots, place, windows, attended, mine, other)


def shards(grid, keep_list, ln_gain, ln_bias, w_qkv, w_out):
    z, core, y, x = (lax.axis_index(name) for name in ("z", "c", "y", "x"))
    place = jnp.stack([z, core, y, x]).astype(jnp.int32)
    slots = keep_list[0, 0]
    windows = grid.reshape(WINDOWS, 4, D)

    swap = lambda array: lax.ppermute(array, "c", ring(2, 1))
    piece = quarter_of(place, jnp.swapaxes(w_qkv, 1, 2))
    heads = lax.all_gather(piece, ("z", "x"), axis=0)

    slots_after = lax.optimization_barrier((slots, piece))[0]
    normed = normed_tokens(
        slots_after, place, windows, ln_gain.reshape(TILES, 128), ln_bias.reshape(TILES, 128)
    )
    own = jnp.concatenate(
        [normed[0]] + [lax.ppermute(normed[shift], "z", ring(4, shift)) for shift in (1, 2, 3)],
        axis=0,
    )
    below = lax.ppermute(own, "y", ring(4, 1))
    above = lax.ppermute(own, "y", ring(4, 3))
    far_top = lax.ppermute(below[: BLOCK // 2], "y", ring(4, 1))
    far_bottom = lax.ppermute(above[BLOCK // 2 :], "y", ring(4, 3))

    eighth = lax.dynamic_slice(w_out, (core * 80, z * 640), (80, 640))
    row = jnp.stack([eighth] + [lax.ppermute(eighth, "x", ring(4, shift)) for shift in (1, 2, 3)])
    row = lax.optimization_barrier((row, far_top, far_bottom))[0]
    w_out_mine = lax.all_gather(row, ("z", "y"), axis=0)

    tokens = [own, below, above, far_top, far_bottom]
    tokens = tokens + [swap(part) for part in tokens]
    to_next, to_far, to_last = project(place, tokens, heads, (1, 2, 3))
    tokens = lax.optimization_barrier((*tokens, to_far))[:10]
    (to_own,) = project(place, tokens, heads, (0,))
    local = [
        to_own,
        lax.ppermute(to_next, "x", ring(4, 1)),
        lax.ppermute(to_far, "x", ring(4, 2)),
        lax.ppermute(to_last, "x", ring(4, 3)),
    ]
    attended = attend(place, local + [swap(part) for part in local])
    w_out_mine = lax.optimization_barrier((w_out_mine, attended))[0]
    w_out_other = swap(w_out_mine)
    attended = lax.all_to_all(attended, ("z", "y", "x"), 0, 0, tiled=True)
    result = finish(slots, place, windows, attended, w_out_mine, w_out_other)
    return result.reshape(grid.shape)


def solution(mesh):
    split = Mesh(mesh.devices.reshape(4, 2, 4, 4), ("z", "c", "y", "x"))
    lat, lon = ("z", "c"), ("y", "x")
    placed = (
        P(lat, lon, None, None),
        P(lat, lon, None),
        P(),
        P(),
        P(lon, None, None),
        P(lon, None),
    )
    return jax.shard_map(
        shards, mesh=split, in_specs=placed, out_specs=P(lat, lon, None, None), check_vma=False
    )
```

```python
import functools
import math

import jax
import jax.numpy as jnp
from jax import lax
from jax.experimental import pallas as pl
from jax.experimental.pallas import tpu as pltpu
from jax.sharding import Mesh
from jax.sharding import PartitionSpec as P

EPSILON = 1e-05
SLOTS = 40
WINDOWS = 64
D = 2560
TILES = D // 128
HD = 160
BLOCK = 4 * SLOTS
COLUMN = 4 * BLOCK
QUERIES = 320
MASKED = -1e30
UNUSED = 1024.0
VMEM_LIMIT = 60 * 1024 * 1024
HALVES = ((0, 32), (64, 96), (160, 192), (224, 256), (320, 352), (384, 416), (128, 288), (448, 0))
BF16 = jnp.bfloat16
F32 = jnp.float32
ANY = pl.BlockSpec(memory_space=pl.ANY)
VMEM = pl.BlockSpec(memory_space=pltpu.VMEM)
SMEM = pl.BlockSpec(memory_space=pltpu.SMEM)


def ring(size, shift):
    return [(i, (i + shift) % size) for i in range(size)]


def params():
    return pltpu.CompilerParams(vmem_limit_bytes=VMEM_LIMIT)


def normed_kernel(slots, place, grid_ref, gain_ref, bias_ref, *refs):
    gain = jnp.concatenate([gain_ref[tile : tile + 1, :] for tile in range(TILES)], axis=1)
    bias = jnp.concatenate([bias_ref[tile : tile + 1, :] for tile in range(TILES)], axis=1)
    outs, tokens = refs[:4], refs[4]
    used = jnp.int32(0)
    for slot in range(SLOTS):
        window = slots[slot]
        used += (window >= 0).astype(jnp.int32)
        loaded = grid_ref[jnp.maximum(window, 0)].astype(F32)
        for tile in range(TILES):
            tokens[tile, pl.ds(4 * slot, 4), :] = loaded[:, tile * 128 : (tile + 1) * 128]
    kept = lax.broadcasted_iota(jnp.int32, (SLOTS, 1), 0) < used
    for shift in range(4):
        position = lax.rem(place[0] + shift, 4)
        values = jnp.concatenate(
            [tokens[tile, pl.ds(position, SLOTS, stride=4), :] for tile in range(TILES)], axis=1
        )
        center = jnp.mean(values, axis=1, keepdims=True)
        moved = values - center
        variance = jnp.mean(moved * moved, axis=1, keepdims=True)
        normed = moved * lax.rsqrt(variance + EPSILON) * gain + bias
        outs[shift][...] = jnp.where(kept, normed, UNUSED).astype(BF16)


def normed_tokens(slots, place, windows, gain, bias):
    return pl.pallas_call(
        normed_kernel,
        out_shape=[jax.ShapeDtypeStruct((SLOTS, D), BF16)] * 4,
        in_specs=[SMEM, SMEM, VMEM, VMEM, VMEM],
        out_specs=[VMEM] * 4,
        scratch_shapes=[pltpu.VMEM((TILES, 4 * SLOTS, 128), F32)],
        compiler_params=params(),
        name="normed",
    )(slots, place, windows, gain, bias)


def piece_kernel(place, raw, piece, sems):
    quarter = 4 * place[1] + place[0]
    for part in range(2):
        first = jnp.int32(HALVES[0][part])
        for i in range(1, 8):
            first = jnp.where(quarter == i, HALVES[i][part], first)
        pltpu.make_async_copy(
            raw.at[0, pl.ds(pl.multiple_of(first, 32), 32)],
            piece.at[pl.ds(32 * part, 32)],
            sems.at[part],
        ).start()
    for part in range(2):
        pltpu.make_async_copy(
            raw.at[0, pl.ds(0, 32)], piece.at[pl.ds(32 * part, 32)], sems.at[part]
        ).wait()


def quarter_of(place, raw):
    return pl.pallas_call(
        piece_kernel,
        out_shape=jax.ShapeDtypeStruct((64, D), BF16),
        in_specs=[SMEM, ANY],
        out_specs=VMEM,
        scratch_shapes=[pltpu.SemaphoreType.DMA((2,))],
        compiler_params=params(),
        name="quarter",
    )(place, raw)


def project_kernel(rows, shifts, place, *refs):
    count, heads = len(rows), len(shifts)
    pieces, weights, refs = refs[:count], refs[count], refs[count + 1 :]
    outs, (tokens, held, token_sems, weight_sems) = refs[:heads], refs[heads:]
    token_copies = []
    total = 0
    for i in range(count):
        token_copies.append(
            pltpu.make_async_copy(pieces[i], tokens.at[pl.ds(total, rows[i])], token_sems.at[i])
        )
        total += rows[i]
    weight_copies = [
        [
            pltpu.make_async_copy(
                weights.at[4 * plane + lax.rem(place[3] + shift, 4)],
                held.at[pl.ds(256 * head + 64 * plane, 64)],
                weight_sems.at[4 * head + plane],
            )
            for plane in range(4)
        ]
        for head, shift in enumerate(shifts)
    ]
    for copy in [copy for made in weight_copies for copy in made] + token_copies:
        copy.start()
    for made in weight_copies:
        for copy in made:
            copy.wait()
    lane = lax.broadcasted_iota(jnp.int32, (COLUMN, 128), 1)
    flagged = (lane >= 96) & (place[1] == 1)
    waited = 0
    for start in range(0, total, COLUMN):
        stop = start + COLUMN
        while waited < count and sum(rows[:waited]) < stop:
            token_copies[waited].wait()
            waited += 1
        chunk = tokens[start:stop]
        mask = jnp.where(chunk[:, 0:128].astype(F32)[:, 0:1] > UNUSED / 2, MASKED, 0.0)
        flags = jnp.where(lane == 96, mask, jnp.where(lane == 97, 1.0, 0.0))
        result = lax.dot_general(
            chunk, held[...], (((1,), (1,)), ((), ())), preferred_element_type=F32
        )
        for head in range(heads):
            base = 256 * head
            outs[head][start:stop, 0:128] = result[:, base : base + 128].astype(BF16)
            outs[head][start:stop, 128:256] = jnp.where(
                flagged, flags, result[:, base + 128 : base + 256]
            ).astype(BF16)


def project(place, pieces, weights, shifts):
    rows = tuple(piece.shape[0] for piece in pieces)
    total, heads = sum(rows), len(shifts)
    return pl.pallas_call(
        functools.partial(project_kernel, rows, shifts),
        out_shape=[jax.ShapeDtypeStruct((total, 256), BF16)] * heads,
        in_specs=[SMEM] + [ANY] * (len(pieces) + 1),
        out_specs=[VMEM] * heads,
        scratch_shapes=[
            pltpu.VMEM((total, D), BF16),
            pltpu.VMEM((heads * 256, D), BF16),
            pltpu.SemaphoreType.DMA((len(pieces),)),
            pltpu.SemaphoreType.DMA((4 * heads,)),
        ],
        compiler_params=params(),
        cost_estimate=pl.CostEstimate(
            flops=2 * total * D * 256 * heads,
            bytes_accessed=total * D * 2 + D * 512 * heads,
            transcendentals=0,
        ),
        name="project",
    )(place, *pieces, weights)


def attend_kernel(first, place, *refs):
    count = 3 if first else 4
    sources, refs = refs[: 2 * count], refs[2 * count :]
    if first:
        sums, tops, held, turned, scores, sems = refs
    else:
        sums, tops, out, held, turned, scores, sems = refs
    near, far = [i for i in range(2 * count) if i % count < 3], [3, 7]
    copies = []
    for i in range(2 * count):
        step, foreign = i % count, i // count
        copies.append([])
        for side in range(2):
            base = pl.multiple_of((1 - place[1] if side else place[1]) * 256, 256)
            copies[i].append(
                pltpu.make_async_copy(
                    sources[count * side + step].at[pl.ds(COLUMN * (foreign ^ side), COLUMN)],
                    held.at[i, :, pl.ds(base, 256)],
                    sems.at[2 * i + side],
                )
            )
    for i in near if first else far + near:
        for copy in copies[i]:
            copy.start()
    lane = lax.broadcasted_iota(jnp.int32, (QUERIES, 128), 1)
    scale = math.log2(math.e) / HD**0.5

    def arrive(piece):
        for copy in copies[piece]:
            copy.wait()

    def turn(piece):
        turned[piece, 0:128, :] = held[piece, :, 128:256].T
        turned[piece, 128:256, :] = held[piece, :, 384:512].T

    def queries_of(index):
        step, half = divmod(index, 2)
        rows = pl.ds(half * QUERIES, QUERIES)
        tail = pltpu.roll(held[step, rows, 384:512].astype(F32), 32, 1)
        tail = jnp.where(
            (lane >= 32) & (lane < 64), tail, jnp.where(lane == 96, 1.0, 0.0)
        ).astype(BF16)
        return jnp.concatenate([held[step, rows, 0:128], tail], axis=1)

    def score(queries, slot, place_, piece, top):
        result = jnp.dot(queries, turned[piece], preferred_element_type=F32)
        scores[slot, :, place_ * COLUMN : (place_ + 1) * COLUMN] = result
        for tile in range(COLUMN // 128):
            part = result[:, tile * 128 : (tile + 1) * 128]
            top = part if top is None else jnp.maximum(top, part)
        return top

    def weigh(slot, place_, piece, peak, total):
        weights = jnp.exp2(
            (scores[slot, :, place_ * COLUMN : (place_ + 1) * COLUMN] - peak) * scale
        ).astype(BF16)
        values = jnp.concatenate([held[piece, :, 256:384], held[piece, :, 384:512]], axis=1)
        result = jnp.dot(weights, values, preferred_element_type=F32)
        return result if total is None else total + result

    def carried(index, peak):
        before = tops[index][:, 0:1]
        joint = jnp.maximum(peak, before)
        return joint, sums[index] * jnp.exp2((before - joint) * scale)

    def keep(index, peak, total):
        sums[index] = total
        tops[index] = jnp.broadcast_to(peak, (QUERIES, 128))

    def emit(index, peak, total):
        step, half = divmod(index, 2)
        x_shift = (0, 1, 3, 2)[step]
        inverse = 1.0 / total[:, 225:226]
        start = total[:, 0:128] * inverse
        last = pltpu.roll(total[:, 128:256] * inverse, 64, 1)
        last = jnp.where(lane < 32, last, 0.0)
        attended = jnp.concatenate([start, last], axis=1)
        for part in range(8):
            y_shift = half * 3 if part < 4 else 1 + half
            target = (
                lax.rem(place[0] + 4 - part % 4, 4) * 16
                + lax.rem(place[2] + 4 - y_shift, 4) * 4
                + lax.rem(place[3] + 4 - x_shift, 4)
            )
            out[target] = attended[part * SLOTS : (part + 1) * SLOTS].astype(BF16)

    def alone(index, peak):
        return peak, None

    if first:
        blocks = [(index, near, alone, keep) for index in range(6)]
        turns = {}
    else:
        blocks = [(index, far, carried, emit) for index in range(6)]
        blocks += [(index, near + far, alone, emit) for index in (6, 7)]
        turns = {0: near[:2], 1: near[2:3], 2: near[3:4], 3: near[4:5], 4: near[5:]}
        for piece in far + near:
            arrive(piece)
        for piece in far:
            turn(piece)
    top, queries = None, None
    for i, piece in enumerate(blocks[0][1]):
        if first:
            arrive(piece)
            turn(piece)
        queries = queries_of(0) if queries is None else queries
        top = score(queries, 0, i, piece, top)
    for number, (index, pieces, begin, end) in enumerate(blocks):
        peak, total = begin(index, jnp.max(top, axis=1, keepdims=True))
        for piece in turns.get(number, ()):
            turn(piece)
        ahead = ()
        if number + 1 < len(blocks):
            ahead, queries, top = blocks[number + 1][1], queries_of(blocks[number + 1][0]), None
        for i in range(max(len(pieces), len(ahead))):
            if i < len(ahead):
                top = score(queries, (number + 1) % 2, i, ahead[i], top)
            if i < len(pieces):
                total = weigh(number % 2, i, pieces[i], peak, total)
        end(index, peak, total)


def attend(place, sources, state=None):
    first = state is None
    pieces = len(sources)
    sums = jax.ShapeDtypeStruct((6, QUERIES, 256), F32)
    tops = jax.ShapeDtypeStruct((6, QUERIES, 128), F32)
    whole = jax.ShapeDtypeStruct((64, SLOTS, 256), BF16)
    work = 9 if first else 7
    return pl.pallas_call(
        functools.partial(attend_kernel, first),
        out_shape=[sums, tops] if first else whole,
        in_specs=[SMEM] + [ANY] * pieces + ([] if first else [VMEM, VMEM]),
        out_specs=[VMEM, VMEM] if first else VMEM,
        scratch_shapes=[
            pltpu.VMEM((pieces, COLUMN, 512), BF16),
            pltpu.VMEM((pieces, 256, COLUMN), BF16),
            pltpu.VMEM((2, QUERIES, pieces * COLUMN), F32),
            pltpu.SemaphoreType.DMA((2 * pieces,)),
        ],
        compiler_params=params(),
        cost_estimate=pl.CostEstimate(
            flops=2 * COLUMN * COLUMN * 4 * 256 * work,
            bytes_accessed=pieces * COLUMN * 1024,
            transcendentals=2 * COLUMN * COLUMN * work,
        ),
        name="attend",
    )(place, *sources, *(state or ()))


def finish_kernel(slots, place, grid_ref, attended, mine, other, out, weights, rows, mixed, sems):
    def copies(core):
        return [
            pltpu.make_async_copy(
                (mine, other)[side].at[pl.ds(4 * plane, 4), shift],
                weights.at[
                    :,
                    lax.rem(place[3] + 4 - shift, 4),
                    pl.ds(80 * (side ^ core), 80),
                    pl.ds(640 * plane, 640),
                ],
                sems.at[8 * plane + 4 * side + shift],
            )
            for plane in range(4)
            for side in range(2)
            for shift in range(4)
        ]

    @pl.when(place[1] == 0)
    def _():
        for copy in copies(0):
            copy.start()

    @pl.when(place[1] == 1)
    def _():
        for copy in copies(1):
            copy.start()

    out[...] = jnp.zeros_like(out)
    for head in range(16):
        stacked = jnp.concatenate(
            [attended[position * 16 + head].astype(F32) for position in range(4)], axis=0
        )
        rows[head] = stacked.astype(BF16)
    for plane in range(4):
        for copy in copies(0)[8 * plane : 8 * plane + 8]:
            copy.wait()
        for start, width in ((0, 256), (256, 256), (512, 128)):
            column = 640 * plane + start
            total = jnp.zeros((BLOCK, width), F32)
            for head in range(16):
                partial = jnp.dot(
                    rows[head, :, 0:HD],
                    weights[head // 4, head % 4, :, column : column + width],
                    preferred_element_type=F32,
                )
                total += partial.astype(BF16).astype(F32)
            for tile in range(width // 128):
                mixed[column // 128 + tile] = total[:, tile * 128 : (tile + 1) * 128]
    for slot in range(SLOTS):
        window = slots[slot]

        @pl.when(window >= 0)
        def _():
            term = jnp.concatenate(
                [mixed[tile, pl.ds(slot, 4, stride=SLOTS), :] for tile in range(TILES)], axis=1
            )
            out[window] = (grid_ref[window].astype(F32) + term).astype(BF16)


def finish(slots, place, windows, attended, mine, other):
    return pl.pallas_call(
        finish_kernel,
        out_shape=jax.ShapeDtypeStruct((WINDOWS, 4, D), BF16),
        in_specs=[SMEM, SMEM, VMEM, VMEM, ANY, ANY],
        out_specs=VMEM,
        scratch_shapes=[
            pltpu.VMEM((4, 4, HD, D), BF16),
            pltpu.VMEM((16, BLOCK, 256), BF16),
            pltpu.VMEM((TILES, BLOCK, 128), F32),
            pltpu.SemaphoreType.DMA((32,)),
        ],
        compiler_params=params(),
        cost_estimate=pl.CostEstimate(
            flops=2 * BLOCK * D * D, bytes_accessed=2 * D * D, transcendentals=0
        ),
        name="finish",
    )(slots, place, windows, attended, mine, other)


def shards(grid, keep_list, ln_gain, ln_bias, w_qkv, w_out):
    z, core, y, x = (lax.axis_index(name) for name in ("z", "c", "y", "x"))
    place = jnp.stack([z, core, y, x]).astype(jnp.int32)
    slots = keep_list[0, 0]
    windows = grid.reshape(WINDOWS, 4, D)

    swap = lambda array: lax.ppermute(array, "c", ring(2, 1))
    piece = quarter_of(place, jnp.swapaxes(w_qkv, 1, 2))
    heads = lax.all_gather(piece, ("z", "x"), axis=0)

    slots_after = lax.optimization_barrier((slots, piece))[0]
    normed = normed_tokens(
        slots_after, place, windows, ln_gain.reshape(TILES, 128), ln_bias.reshape(TILES, 128)
    )
    own = jnp.concatenate(
        [normed[0]] + [lax.ppermute(normed[shift], "z", ring(4, shift)) for shift in (1, 2, 3)],
        axis=0,
    )
    below = lax.ppermute(own, "y", ring(4, 1))
    above = lax.ppermute(own, "y", ring(4, 3))
    far_top = lax.ppermute(below[: BLOCK // 2], "y", ring(4, 1))
    far_bottom = lax.ppermute(above[BLOCK // 2 :], "y", ring(4, 3))

    eighth = lax.dynamic_slice(w_out, (core * 80, z * 640), (80, 640))
    row = jnp.stack([eighth] + [lax.ppermute(eighth, "x", ring(4, shift)) for shift in (1, 2, 3)])
    row = lax.optimization_barrier((row, far_top, far_bottom))[0]
    w_out_mine = lax.all_gather(row, ("z", "y"), axis=0)

    tokens = [own, below, above, far_top, far_bottom]
    tokens = tokens + [swap(part) for part in tokens]
    to_next, to_far, to_last = project(place, tokens, heads, (1, 2, 3))
    tokens = lax.optimization_barrier((*tokens, to_far))[:10]
    (to_own,) = project(place, tokens, heads, (0,))
    local = [to_own, lax.ppermute(to_next, "x", ring(4, 1)), lax.ppermute(to_last, "x", ring(4, 3))]
    remote = [swap(part) for part in local]
    from_far = lax.ppermute(to_far, "x", ring(4, 2))
    state = attend(place, local + remote)
    from_far = lax.optimization_barrier((from_far, *state))[0]
    attended = attend(place, local + [from_far] + remote + [swap(from_far)], state)
    w_out_mine = lax.optimization_barrier((w_out_mine, attended))[0]
    w_out_other = swap(w_out_mine)
    attended = lax.all_to_all(attended, ("z", "y", "x"), 0, 0, tiled=True)
    result = finish(slots, place, windows, attended, w_out_mine, w_out_other)
    return result.reshape(grid.shape)


def solution(mesh):
    split = Mesh(mesh.devices.reshape(4, 2, 4, 4), ("z", "c", "y", "x"))
    lat, lon = ("z", "c"), ("y", "x")
    placed = (
        P(lat, lon, None, None),
        P(lat, lon, None),
        P(),
        P(),
        P(lon, None, None),
        P(lon, None),
    )
    return jax.shard_map(
        shards, mesh=split, in_specs=placed, out_specs=P(lat, lon, None, None), check_vma=False
    )
```

```python
import functools
import math

import jax
import jax.numpy as jnp
from jax import lax
from jax.experimental import pallas as pl
from jax.experimental.pallas import tpu as pltpu
from jax.sharding import Mesh
from jax.sharding import PartitionSpec as P

EPSILON = 1e-05
SLOTS = 40
WINDOWS = 64
D = 2560
TILES = D // 128
HD = 160
BLOCK = 4 * SLOTS
COLUMN = 4 * BLOCK
QUERIES = 320
MASKED = -1e30
UNUSED = 1024.0
VMEM_LIMIT = 60 * 1024 * 1024
HALVES = ((0, 32), (64, 96), (160, 192), (224, 256), (320, 352), (384, 416), (128, 288), (448, 0))
BF16 = jnp.bfloat16
F32 = jnp.float32
ANY = pl.BlockSpec(memory_space=pl.ANY)
VMEM = pl.BlockSpec(memory_space=pltpu.VMEM)
SMEM = pl.BlockSpec(memory_space=pltpu.SMEM)


def ring(size, shift):
    return [(i, (i + shift) % size) for i in range(size)]


def params():
    return pltpu.CompilerParams(vmem_limit_bytes=VMEM_LIMIT)


def normed_kernel(slots, place, grid_ref, gain_ref, bias_ref, *refs):
    gain = jnp.concatenate([gain_ref[tile : tile + 1, :] for tile in range(TILES)], axis=1)
    bias = jnp.concatenate([bias_ref[tile : tile + 1, :] for tile in range(TILES)], axis=1)
    outs, tokens = refs[:4], refs[4]
    used = jnp.int32(0)
    for slot in range(SLOTS):
        window = slots[slot]
        used += (window >= 0).astype(jnp.int32)
        loaded = grid_ref[jnp.maximum(window, 0)].astype(F32)
        for tile in range(TILES):
            tokens[tile, pl.ds(4 * slot, 4), :] = loaded[:, tile * 128 : (tile + 1) * 128]
    kept = lax.broadcasted_iota(jnp.int32, (SLOTS, 1), 0) < used
    for shift in range(4):
        position = lax.rem(place[0] + shift, 4)
        values = jnp.concatenate(
            [tokens[tile, pl.ds(position, SLOTS, stride=4), :] for tile in range(TILES)], axis=1
        )
        center = jnp.mean(values, axis=1, keepdims=True)
        moved = values - center
        variance = jnp.mean(moved * moved, axis=1, keepdims=True)
        normed = moved * lax.rsqrt(variance + EPSILON) * gain + bias
        outs[shift][...] = jnp.where(kept, normed, UNUSED).astype(BF16)


def normed_tokens(slots, place, windows, gain, bias):
    return pl.pallas_call(
        normed_kernel,
        out_shape=[jax.ShapeDtypeStruct((SLOTS, D), BF16)] * 4,
        in_specs=[SMEM, SMEM, VMEM, VMEM, VMEM],
        out_specs=[VMEM] * 4,
        scratch_shapes=[pltpu.VMEM((TILES, 4 * SLOTS, 128), F32)],
        compiler_params=params(),
        name="normed",
    )(slots, place, windows, gain, bias)


def piece_kernel(place, raw, piece, sems):
    quarter = 4 * place[1] + place[0]
    for part in range(2):
        first = jnp.int32(HALVES[0][part])
        for i in range(1, 8):
            first = jnp.where(quarter == i, HALVES[i][part], first)
        pltpu.make_async_copy(
            raw.at[0, pl.ds(pl.multiple_of(first, 32), 32)],
            piece.at[pl.ds(32 * part, 32)],
            sems.at[part],
        ).start()
    for part in range(2):
        pltpu.make_async_copy(
            raw.at[0, pl.ds(0, 32)], piece.at[pl.ds(32 * part, 32)], sems.at[part]
        ).wait()


def quarter_of(place, raw):
    return pl.pallas_call(
        piece_kernel,
        out_shape=jax.ShapeDtypeStruct((64, D), BF16),
        in_specs=[SMEM, ANY],
        out_specs=VMEM,
        scratch_shapes=[pltpu.SemaphoreType.DMA((2,))],
        compiler_params=params(),
        name="quarter",
    )(place, raw)


def project_kernel(rows, shifts, place, *refs):
    count, heads = len(rows), len(shifts)
    pieces, weights, refs = refs[:count], refs[count], refs[count + 1 :]
    outs, (tokens, held, token_sems, weight_sems) = refs[:heads], refs[heads:]
    token_copies = []
    total = 0
    for i in range(count):
        token_copies.append(
            pltpu.make_async_copy(pieces[i], tokens.at[pl.ds(total, rows[i])], token_sems.at[i])
        )
        total += rows[i]
    weight_copies = [
        [
            pltpu.make_async_copy(
                weights.at[4 * plane + lax.rem(place[3] + shift, 4)],
                held.at[pl.ds(256 * head + 64 * plane, 64)],
                weight_sems.at[4 * head + plane],
            )
            for plane in range(4)
        ]
        for head, shift in enumerate(shifts)
    ]
    for copy in [copy for made in weight_copies for copy in made] + token_copies:
        copy.start()
    for made in weight_copies:
        for copy in made:
            copy.wait()
    lane = lax.broadcasted_iota(jnp.int32, (COLUMN, 128), 1)
    flagged = (lane >= 96) & (place[1] == 1)
    waited = 0
    for start in range(0, total, COLUMN):
        stop = start + COLUMN
        while waited < count and sum(rows[:waited]) < stop:
            token_copies[waited].wait()
            waited += 1
        chunk = tokens[start:stop]
        mask = jnp.where(chunk[:, 0:128].astype(F32)[:, 0:1] > UNUSED / 2, MASKED, 0.0)
        flags = jnp.where(lane == 96, mask, jnp.where(lane == 97, 1.0, 0.0))
        result = lax.dot_general(
            chunk, held[...], (((1,), (1,)), ((), ())), preferred_element_type=F32
        )
        for head in range(heads):
            base = 256 * head
            outs[head][start:stop, 0:128] = result[:, base : base + 128].astype(BF16)
            outs[head][start:stop, 128:256] = jnp.where(
                flagged, flags, result[:, base + 128 : base + 256]
            ).astype(BF16)


def project(place, pieces, weights, shifts):
    rows = tuple(piece.shape[0] for piece in pieces)
    total, heads = sum(rows), len(shifts)
    return pl.pallas_call(
        functools.partial(project_kernel, rows, shifts),
        out_shape=[jax.ShapeDtypeStruct((total, 256), BF16)] * heads,
        in_specs=[SMEM] + [ANY] * (len(pieces) + 1),
        out_specs=[VMEM] * heads,
        scratch_shapes=[
            pltpu.VMEM((total, D), BF16),
            pltpu.VMEM((heads * 256, D), BF16),
            pltpu.SemaphoreType.DMA((len(pieces),)),
            pltpu.SemaphoreType.DMA((4 * heads,)),
        ],
        compiler_params=params(),
        cost_estimate=pl.CostEstimate(
            flops=2 * total * D * 256 * heads,
            bytes_accessed=total * D * 2 + D * 512 * heads,
            transcendentals=0,
        ),
        name="project",
    )(place, *pieces, weights)


def attend_kernel(first, place, *refs):
    count = 3 if first else 4
    sources, refs = refs[: 2 * count], refs[2 * count :]
    if first:
        sums, tops, held, turned, scores, sems = refs
    else:
        sums, tops, out, held, turned, scores, sems = refs
    near, far = [i for i in range(2 * count) if i % count < 3], [3, 7]
    copies = []
    for i in range(2 * count):
        step, foreign = i % count, i // count
        copies.append([])
        for side in range(2):
            base = pl.multiple_of((1 - place[1] if side else place[1]) * 256, 256)
            copies[i].append(
                pltpu.make_async_copy(
                    sources[count * side + step].at[pl.ds(COLUMN * (foreign ^ side), COLUMN)],
                    held.at[i, :, pl.ds(base, 256)],
                    sems.at[2 * i + side],
                )
            )
    for i in near if first else far + near:
        for copy in copies[i]:
            copy.start()
    lane = lax.broadcasted_iota(jnp.int32, (QUERIES, 128), 1)
    scale = math.log2(math.e) / HD**0.5

    def arrive(piece):
        for copy in copies[piece]:
            copy.wait()

    def turn(piece):
        turned[piece, 0:128, :] = held[piece, :, 128:256].T
        turned[piece, 128:256, :] = held[piece, :, 384:512].T

    def queries_of(index):
        step, half = divmod(index, 2)
        rows = pl.ds(half * QUERIES, QUERIES)
        tail = pltpu.roll(held[step, rows, 384:512].astype(F32), 32, 1)
        tail = jnp.where(
            (lane >= 32) & (lane < 64), tail, jnp.where(lane == 96, 1.0, 0.0)
        ).astype(BF16)
        return jnp.concatenate([held[step, rows, 0:128], tail], axis=1)

    def score(queries, slot, place_, piece, top):
        result = jnp.dot(queries, turned[piece], preferred_element_type=F32)
        scores[slot, :, place_ * COLUMN : (place_ + 1) * COLUMN] = result
        for tile in range(COLUMN // 128):
            part = result[:, tile * 128 : (tile + 1) * 128]
            top = part if top is None else jnp.maximum(top, part)
        return top

    def weigh(slot, place_, piece, peak, total):
        weights = jnp.exp2(
            (scores[slot, :, place_ * COLUMN : (place_ + 1) * COLUMN] - peak) * scale
        ).astype(BF16)
        values = jnp.concatenate([held[piece, :, 256:384], held[piece, :, 384:512]], axis=1)
        result = jnp.dot(weights, values, preferred_element_type=F32)
        return result if total is None else total + result

    def carried(index, peak):
        before = tops[index][:, 0:1]
        joint = jnp.maximum(peak, before)
        return joint, sums[index] * jnp.exp2((before - joint) * scale)

    def keep(index, peak, total):
        sums[index] = total
        tops[index] = jnp.broadcast_to(peak, (QUERIES, 128))

    def emit(index, peak, total):
        step, half = divmod(index, 2)
        x_shift = (0, 1, 3, 2)[step]
        inverse = 1.0 / total[:, 225:226]
        start = total[:, 0:128] * inverse
        last = pltpu.roll(total[:, 128:256] * inverse, 64, 1)
        last = jnp.where(lane < 32, last, 0.0)
        attended = jnp.concatenate([start, last], axis=1)
        for part in range(8):
            y_shift = half * 3 if part < 4 else 1 + half
            target = (
                lax.rem(place[0] + 4 - part % 4, 4) * 16
                + lax.rem(place[2] + 4 - y_shift, 4) * 4
                + lax.rem(place[3] + 4 - x_shift, 4)
            )
            out[target] = attended[part * SLOTS : (part + 1) * SLOTS].astype(BF16)

    def alone(index, peak):
        return peak, None

    if first:
        blocks = [(index, near, alone, keep) for index in range(6)]
        turns = {}
    else:
        blocks = [(index, far, carried, emit) for index in range(6)]
        blocks += [(index, near + far, alone, emit) for index in (6, 7)]
        turns = {0: near[:2], 1: near[2:3], 2: near[3:4], 3: near[4:5], 4: near[5:]}
        for piece in far + near:
            arrive(piece)
        for piece in far:
            turn(piece)
    top, queries = None, None
    for i, piece in enumerate(blocks[0][1]):
        if first:
            arrive(piece)
            turn(piece)
        queries = queries_of(0) if queries is None else queries
        top = score(queries, 0, i, piece, top)
    for number, (index, pieces, begin, end) in enumerate(blocks):
        peak, total = begin(index, jnp.max(top, axis=1, keepdims=True))
        for piece in turns.get(number, ()):
            turn(piece)
        ahead = ()
        if number + 1 < len(blocks):
            ahead, queries, top = blocks[number + 1][1], queries_of(blocks[number + 1][0]), None
        for i in range(max(len(pieces), len(ahead))):
            if i < len(ahead):
                top = score(queries, (number + 1) % 2, i, ahead[i], top)
            if i < len(pieces):
                total = weigh(number % 2, i, pieces[i], peak, total)
        end(index, peak, total)


def attend(place, sources, state=None):
    first = state is None
    pieces = len(sources)
    sums = jax.ShapeDtypeStruct((6, QUERIES, 256), F32)
    tops = jax.ShapeDtypeStruct((6, QUERIES, 128), F32)
    whole = jax.ShapeDtypeStruct((64, SLOTS, 256), BF16)
    work = 9 if first else 7
    return pl.pallas_call(
        functools.partial(attend_kernel, first),
        out_shape=[sums, tops] if first else whole,
        in_specs=[SMEM] + [ANY] * pieces + ([] if first else [VMEM, VMEM]),
        out_specs=[VMEM, VMEM] if first else VMEM,
        scratch_shapes=[
            pltpu.VMEM((pieces, COLUMN, 512), BF16),
            pltpu.VMEM((pieces, 256, COLUMN), BF16),
            pltpu.VMEM((2, QUERIES, pieces * COLUMN), F32),
            pltpu.SemaphoreType.DMA((2 * pieces,)),
        ],
        compiler_params=params(),
        cost_estimate=pl.CostEstimate(
            flops=2 * COLUMN * COLUMN * 4 * 256 * work,
            bytes_accessed=pieces * COLUMN * 1024,
            transcendentals=2 * COLUMN * COLUMN * work,
        ),
        name="attend",
    )(place, *sources, *(state or ()))


def finish_kernel(slots, place, grid_ref, attended, mine, other, out, weights, rows, mixed, sems):
    def copies(core, plane):
        return [
            pltpu.make_async_copy(
                (mine, other)[side].at[pl.ds(4 * plane, 4), shift],
                weights.at[
                    :,
                    lax.rem(place[3] + 4 - shift, 4),
                    pl.ds(80 * (side ^ core), 80),
                    pl.ds(640 * plane, 640),
                ],
                sems.at[8 * plane + 4 * side + shift],
            )
            for side in range(2)
            for shift in range(4)
        ]

    def fetch(plane):
        for core in range(2):

            @pl.when(place[1] == core)
            def _():
                for copy in copies(core, plane):
                    copy.start()

    fetch(0)
    fetch(1)
    out[...] = jnp.zeros_like(out)
    for head in range(16):
        stacked = jnp.concatenate(
            [attended[position * 16 + head].astype(F32) for position in range(4)], axis=0
        )
        rows[head] = stacked.astype(BF16)
    for plane in range(4):
        for copy in copies(0, plane):
            copy.wait()
        if plane < 2:
            fetch(plane + 2)
        for start, width in ((0, 256), (256, 256), (512, 128)):
            column = 640 * plane + start
            total = jnp.zeros((BLOCK, width), F32)
            for head in range(16):
                partial = jnp.dot(
                    rows[head, :, 0:HD],
                    weights[head // 4, head % 4, :, column : column + width],
                    preferred_element_type=F32,
                )
                total += partial.astype(BF16).astype(F32)
            for tile in range(width // 128):
                mixed[column // 128 + tile] = total[:, tile * 128 : (tile + 1) * 128]
    for slot in range(SLOTS):
        window = slots[slot]

        @pl.when(window >= 0)
        def _():
            term = jnp.concatenate(
                [mixed[tile, pl.ds(slot, 4, stride=SLOTS), :] for tile in range(TILES)], axis=1
            )
            out[window] = (grid_ref[window].astype(F32) + term).astype(BF16)


def finish(slots, place, windows, attended, mine, other):
    return pl.pallas_call(
        finish_kernel,
        out_shape=jax.ShapeDtypeStruct((WINDOWS, 4, D), BF16),
        in_specs=[SMEM, SMEM, VMEM, VMEM, ANY, ANY],
        out_specs=VMEM,
        scratch_shapes=[
            pltpu.VMEM((4, 4, HD, D), BF16),
            pltpu.VMEM((16, BLOCK, 256), BF16),
            pltpu.VMEM((TILES, BLOCK, 128), F32),
            pltpu.SemaphoreType.DMA((32,)),
        ],
        compiler_params=params(),
        cost_estimate=pl.CostEstimate(
            flops=2 * BLOCK * D * D, bytes_accessed=2 * D * D, transcendentals=0
        ),
        name="finish",
    )(slots, place, windows, attended, mine, other)


def shards(grid, keep_list, ln_gain, ln_bias, w_qkv, w_out):
    z, core, y, x = (lax.axis_index(name) for name in ("z", "c", "y", "x"))
    place = jnp.stack([z, core, y, x]).astype(jnp.int32)
    slots = keep_list[0, 0]
    windows = grid.reshape(WINDOWS, 4, D)

    swap = lambda array: lax.ppermute(array, "c", ring(2, 1))
    piece = quarter_of(place, jnp.swapaxes(w_qkv, 1, 2))
    heads = lax.all_gather(piece, ("z", "x"), axis=0)

    slots_after = lax.optimization_barrier((slots, piece))[0]
    normed = normed_tokens(
        slots_after, place, windows, ln_gain.reshape(TILES, 128), ln_bias.reshape(TILES, 128)
    )
    own = jnp.concatenate(
        [normed[0]] + [lax.ppermute(normed[shift], "z", ring(4, shift)) for shift in (1, 2, 3)],
        axis=0,
    )
    below = lax.ppermute(own, "y", ring(4, 1))
    above = lax.ppermute(own, "y", ring(4, 3))
    far_top = lax.ppermute(below[: BLOCK // 2], "y", ring(4, 1))
    far_bottom = lax.ppermute(above[BLOCK // 2 :], "y", ring(4, 3))

    eighth = lax.dynamic_slice(w_out, (core * 80, z * 640), (80, 640))
    row = jnp.stack([eighth] + [lax.ppermute(eighth, "x", ring(4, shift)) for shift in (1, 2, 3)])
    row = lax.optimization_barrier((row, far_top, far_bottom))[0]
    w_out_mine = lax.all_gather(row, ("z", "y"), axis=0)

    tokens = [own, below, above, far_top, far_bottom]
    tokens = tokens + [swap(part) for part in tokens]
    to_next, to_last = project(place, tokens, heads, (1, 3))
    tokens = lax.optimization_barrier((*tokens, to_next))[:10]
    to_far, to_own = project(place, tokens, heads, (2, 0))
    local = [to_own, lax.ppermute(to_next, "x", ring(4, 1)), lax.ppermute(to_last, "x", ring(4, 3))]
    remote = [swap(part) for part in local]
    from_far = lax.ppermute(to_far, "x", ring(4, 2))
    state = attend(place, local + remote)
    from_far = lax.optimization_barrier((from_far, *state))[0]
    attended = attend(place, local + [from_far] + remote + [swap(from_far)], state)
    w_out_mine = lax.optimization_barrier((w_out_mine, attended))[0]
    w_out_other = swap(w_out_mine)
    attended = lax.all_to_all(attended, ("z", "y", "x"), 0, 0, tiled=True)
    result = finish(slots, place, windows, attended, w_out_mine, w_out_other)
    return result.reshape(grid.shape)


def solution(mesh):
    split = Mesh(mesh.devices.reshape(4, 2, 4, 4), ("z", "c", "y", "x"))
    lat, lon = ("z", "c"), ("y", "x")
    placed = (
        P(lat, lon, None, None),
        P(lat, lon, None),
        P(),
        P(),
        P(lon, None, None),
        P(lon, None),
    )
    return jax.shard_map(
        shards, mesh=split, in_specs=placed, out_specs=P(lat, lon, None, None), check_vma=False
    )
```

```python
import functools
import math

import jax
import jax.numpy as jnp
from jax import lax
from jax.experimental import pallas as pl
from jax.experimental.pallas import tpu as pltpu
from jax.sharding import Mesh
from jax.sharding import PartitionSpec as P

EPSILON = 1e-05
SLOTS = 40
WINDOWS = 64
D = 2560
TILES = D // 128
HD = 160
BLOCK = 4 * SLOTS
COLUMN = 4 * BLOCK
QUERIES = 320
MASKED = -1e30
UNUSED = 1024.0
VMEM_LIMIT = 60 * 1024 * 1024
HALVES = ((0, 32), (64, 96), (160, 192), (224, 256), (320, 352), (384, 416), (128, 288), (448, 0))
BF16 = jnp.bfloat16
F32 = jnp.float32
ANY = pl.BlockSpec(memory_space=pl.ANY)
VMEM = pl.BlockSpec(memory_space=pltpu.VMEM)
SMEM = pl.BlockSpec(memory_space=pltpu.SMEM)


def ring(size, shift):
    return [(i, (i + shift) % size) for i in range(size)]


def params():
    return pltpu.CompilerParams(vmem_limit_bytes=VMEM_LIMIT)


def normed_kernel(slots, place, grid_ref, gain_ref, bias_ref, *refs):
    gain = jnp.concatenate([gain_ref[tile : tile + 1, :] for tile in range(TILES)], axis=1)
    bias = jnp.concatenate([bias_ref[tile : tile + 1, :] for tile in range(TILES)], axis=1)
    outs, tokens = refs[:4], refs[4]
    used = jnp.int32(0)
    for slot in range(SLOTS):
        window = slots[slot]
        used += (window >= 0).astype(jnp.int32)
        loaded = grid_ref[jnp.maximum(window, 0)].astype(F32)
        for tile in range(TILES):
            tokens[tile, pl.ds(4 * slot, 4), :] = loaded[:, tile * 128 : (tile + 1) * 128]
    kept = lax.broadcasted_iota(jnp.int32, (SLOTS, 1), 0) < used
    for shift in range(4):
        position = lax.rem(place[0] + shift, 4)
        values = jnp.concatenate(
            [tokens[tile, pl.ds(position, SLOTS, stride=4), :] for tile in range(TILES)], axis=1
        )
        center = jnp.mean(values, axis=1, keepdims=True)
        moved = values - center
        variance = jnp.mean(moved * moved, axis=1, keepdims=True)
        normed = moved * lax.rsqrt(variance + EPSILON) * gain + bias
        outs[shift][...] = jnp.where(kept, normed, UNUSED).astype(BF16)


def normed_tokens(slots, place, windows, gain, bias):
    return pl.pallas_call(
        normed_kernel,
        out_shape=[jax.ShapeDtypeStruct((SLOTS, D), BF16)] * 4,
        in_specs=[SMEM, SMEM, VMEM, VMEM, VMEM],
        out_specs=[VMEM] * 4,
        scratch_shapes=[pltpu.VMEM((TILES, 4 * SLOTS, 128), F32)],
        compiler_params=params(),
        name="normed",
    )(slots, place, windows, gain, bias)


def piece_kernel(place, raw, piece, sems):
    quarter = 4 * place[1] + place[0]
    for part in range(2):
        first = jnp.int32(HALVES[0][part])
        for i in range(1, 8):
            first = jnp.where(quarter == i, HALVES[i][part], first)
        pltpu.make_async_copy(
            raw.at[0, pl.ds(pl.multiple_of(first, 32), 32)],
            piece.at[pl.ds(32 * part, 32)],
            sems.at[part],
        ).start()
    for part in range(2):
        pltpu.make_async_copy(
            raw.at[0, pl.ds(0, 32)], piece.at[pl.ds(32 * part, 32)], sems.at[part]
        ).wait()


def quarter_of(place, raw):
    return pl.pallas_call(
        piece_kernel,
        out_shape=jax.ShapeDtypeStruct((64, D), BF16),
        in_specs=[SMEM, ANY],
        out_specs=VMEM,
        scratch_shapes=[pltpu.SemaphoreType.DMA((2,))],
        compiler_params=params(),
        name="quarter",
    )(place, raw)


def project_kernel(rows, shifts, place, *refs):
    count, heads = len(rows), len(shifts)
    pieces, weights, refs = refs[:count], refs[count], refs[count + 1 :]
    outs, (tokens, held, token_sems, weight_sems) = refs[:heads], refs[heads:]
    token_copies = []
    total = 0
    for i in range(count):
        token_copies.append(
            pltpu.make_async_copy(pieces[i], tokens.at[pl.ds(total, rows[i])], token_sems.at[i])
        )
        total += rows[i]
    weight_copies = [
        [
            pltpu.make_async_copy(
                weights.at[4 * plane + lax.rem(place[3] + shift, 4)],
                held.at[pl.ds(256 * head + 64 * plane, 64)],
                weight_sems.at[4 * head + plane],
            )
            for plane in range(4)
        ]
        for head, shift in enumerate(shifts)
    ]
    for copy in [copy for made in weight_copies for copy in made] + token_copies:
        copy.start()
    for made in weight_copies:
        for copy in made:
            copy.wait()
    lane = lax.broadcasted_iota(jnp.int32, (COLUMN, 128), 1)
    flagged = (lane >= 96) & (place[1] == 1)
    waited = 0
    for start in range(0, total, COLUMN):
        stop = start + COLUMN
        while waited < count and sum(rows[:waited]) < stop:
            token_copies[waited].wait()
            waited += 1
        chunk = tokens[start:stop]
        mask = jnp.where(chunk[:, 0:128].astype(F32)[:, 0:1] > UNUSED / 2, MASKED, 0.0)
        flags = jnp.where(lane == 96, mask, jnp.where(lane == 97, 1.0, 0.0))
        result = lax.dot_general(
            chunk, held[...], (((1,), (1,)), ((), ())), preferred_element_type=F32
        )
        for head in range(heads):
            base = 256 * head
            outs[head][start:stop, 0:128] = result[:, base : base + 128].astype(BF16)
            outs[head][start:stop, 128:256] = jnp.where(
                flagged, flags, result[:, base + 128 : base + 256]
            ).astype(BF16)


def project(place, pieces, weights, shifts):
    rows = tuple(piece.shape[0] for piece in pieces)
    total, heads = sum(rows), len(shifts)
    return pl.pallas_call(
        functools.partial(project_kernel, rows, shifts),
        out_shape=[jax.ShapeDtypeStruct((total, 256), BF16)] * heads,
        in_specs=[SMEM] + [ANY] * (len(pieces) + 1),
        out_specs=[VMEM] * heads,
        scratch_shapes=[
            pltpu.VMEM((total, D), BF16),
            pltpu.VMEM((heads * 256, D), BF16),
            pltpu.SemaphoreType.DMA((len(pieces),)),
            pltpu.SemaphoreType.DMA((4 * heads,)),
        ],
        compiler_params=params(),
        cost_estimate=pl.CostEstimate(
            flops=2 * total * D * 256 * heads,
            bytes_accessed=total * D * 2 + D * 512 * heads,
            transcendentals=0,
        ),
        name="project",
    )(place, *pieces, weights)


def attend_kernel(first, place, *refs):
    count = 3 if first else 4
    sources, refs = refs[: 2 * count], refs[2 * count :]
    if first:
        sums, tops, held, turned, scores, sems = refs
    else:
        sums, tops, out, held, turned, scores, sems = refs
    near, far = [i for i in range(2 * count) if i % count < 3], [3, 7]
    copies = []
    for i in range(2 * count):
        step, foreign = i % count, i // count
        copies.append([])
        for side in range(2):
            base = pl.multiple_of((1 - place[1] if side else place[1]) * 256, 256)
            copies[i].append(
                pltpu.make_async_copy(
                    sources[count * side + step].at[pl.ds(COLUMN * (foreign ^ side), COLUMN)],
                    held.at[i, :, pl.ds(base, 256)],
                    sems.at[2 * i + side],
                )
            )
    for i in near if first else far + near:
        for copy in copies[i]:
            copy.start()
    lane = lax.broadcasted_iota(jnp.int32, (QUERIES, 128), 1)
    scale = math.log2(math.e) / HD**0.5

    def arrive(piece):
        for copy in copies[piece]:
            copy.wait()

    def turn(piece):
        turned[piece, 0:128, :] = held[piece, :, 128:256].T
        turned[piece, 128:256, :] = held[piece, :, 384:512].T

    def queries_of(index):
        step, half = index // 2, index % 2
        rows = pl.ds(pl.multiple_of(half * QUERIES, QUERIES), QUERIES)
        tail = pltpu.roll(held[step, rows, 384:512].astype(F32), 32, 1)
        tail = jnp.where(
            (lane >= 32) & (lane < 64), tail, jnp.where(lane == 96, 1.0, 0.0)
        ).astype(BF16)
        return jnp.concatenate([held[step, rows, 0:128], tail], axis=1)

    def score(queries, slot, place_, piece, top):
        result = jnp.dot(queries, turned[piece], preferred_element_type=F32)
        scores[slot, :, place_ * COLUMN : (place_ + 1) * COLUMN] = result
        for tile in range(COLUMN // 128):
            part = result[:, tile * 128 : (tile + 1) * 128]
            top = part if top is None else jnp.maximum(top, part)
        return top

    def weigh(slot, place_, piece, peak, total):
        weights = jnp.exp2(
            (scores[slot, :, place_ * COLUMN : (place_ + 1) * COLUMN] - peak) * scale
        ).astype(BF16)
        values = jnp.concatenate([held[piece, :, 256:384], held[piece, :, 384:512]], axis=1)
        result = jnp.dot(weights, values, preferred_element_type=F32)
        return result if total is None else total + result

    def carried(index, peak):
        before = tops[index][:, 0:1]
        joint = jnp.maximum(peak, before)
        return joint, sums[index] * jnp.exp2((before - joint) * scale)

    def keep(index, peak, total):
        sums[index] = total
        tops[index] = jnp.broadcast_to(peak, (QUERIES, 128))

    def emit(index, peak, total):
        step, half = divmod(index, 2)
        x_shift = (0, 1, 3, 2)[step]
        inverse = 1.0 / total[:, 225:226]
        start = total[:, 0:128] * inverse
        last = pltpu.roll(total[:, 128:256] * inverse, 64, 1)
        last = jnp.where(lane < 32, last, 0.0)
        for part in range(8):
            y_shift = half * 3 if part < 4 else 1 + half
            target = (
                lax.rem(place[0] + 4 - part % 4, 4) * 16
                + lax.rem(place[2] + 4 - y_shift, 4) * 4
                + lax.rem(place[3] + 4 - x_shift, 4)
            )
            base = part * SLOTS
            packed = last[base : base + 8]
            for group in range(1, 4):
                rows = last[base + 8 * group : base + 8 * group + 8]
                packed += pltpu.roll(rows, 32 * group, 1)
            out[target] = jnp.concatenate(
                [start[base : base + SLOTS], packed, last[base + 32 : base + SLOTS]], axis=0
            ).astype(BF16)

    def alone(index, peak):
        return peak, None

    if first:
        blocks = [(index, near, alone, keep) for index in range(6)]
        turns = {}
    else:
        blocks = [(index, far, carried, emit) for index in range(6)]
        blocks += [(index, near + far, alone, emit) for index in (6, 7)]
        turns = {0: near[:2], 1: near[2:3], 2: near[3:4], 3: near[4:5], 4: near[5:]}
        for piece in far + near:
            arrive(piece)
        for piece in far:
            turn(piece)
    top, queries = None, None
    for i, piece in enumerate(blocks[0][1]):
        if first:
            arrive(piece)
            turn(piece)
        queries = queries_of(0) if queries is None else queries
        top = score(queries, 0, i, piece, top)
    if first:

        def two_blocks(pair, peak):
            for slot in range(2):
                index = 2 * pair + slot
                queries, top, total = queries_of(jnp.minimum(index + 1, 5)), None, None
                for i, piece in enumerate(near):
                    top = score(queries, 1 - slot, i, piece, top)
                    total = weigh(slot, i, piece, peak, total)
                keep(index, peak, total)
                peak = jnp.max(top, axis=1, keepdims=True)
            return peak

        lax.fori_loop(0, 3, two_blocks, jnp.max(top, axis=1, keepdims=True))
        return
    for number, (index, pieces, begin, end) in enumerate(blocks):
        peak, total = begin(index, jnp.max(top, axis=1, keepdims=True))
        for piece in turns.get(number, ()):
            turn(piece)
        ahead = ()
        if number + 1 < len(blocks):
            ahead, queries, top = blocks[number + 1][1], queries_of(blocks[number + 1][0]), None
        for i in range(max(len(pieces), len(ahead))):
            if i < len(ahead):
                top = score(queries, (number + 1) % 2, i, ahead[i], top)
            if i < len(pieces):
                total = weigh(number % 2, i, pieces[i], peak, total)
        end(index, peak, total)


def attend(place, sources, state=None):
    first = state is None
    pieces = len(sources)
    sums = jax.ShapeDtypeStruct((6, QUERIES, 256), F32)
    tops = jax.ShapeDtypeStruct((6, QUERIES, 128), F32)
    whole = jax.ShapeDtypeStruct((64, SLOTS + 16, 128), BF16)
    work = 9 if first else 7
    return pl.pallas_call(
        functools.partial(attend_kernel, first),
        out_shape=[sums, tops] if first else whole,
        in_specs=[SMEM] + [ANY] * pieces + ([] if first else [VMEM, VMEM]),
        out_specs=[VMEM, VMEM] if first else VMEM,
        scratch_shapes=[
            pltpu.VMEM((pieces, COLUMN, 512), BF16),
            pltpu.VMEM((pieces, 256, COLUMN), BF16),
            pltpu.VMEM((2, QUERIES, pieces * COLUMN), F32),
            pltpu.SemaphoreType.DMA((2 * pieces,)),
        ],
        compiler_params=params(),
        cost_estimate=pl.CostEstimate(
            flops=2 * COLUMN * COLUMN * 4 * 256 * work,
            bytes_accessed=pieces * COLUMN * 1024,
            transcendentals=2 * COLUMN * COLUMN * work,
        ),
        name="attend",
    )(place, *sources, *(state or ()))


def finish_kernel(slots, place, grid_ref, attended, mine, other, out, weights, rows, mixed, sems):
    def copies(core, plane):
        return [
            pltpu.make_async_copy(
                (mine, other)[side].at[pl.ds(4 * plane, 4), shift],
                weights.at[
                    :,
                    lax.rem(place[3] + 4 - shift, 4),
                    pl.ds(80 * (side ^ core), 80),
                    pl.ds(pl.multiple_of(640 * plane, 128), 640),
                ],
                sems.at[8 * plane + 4 * side + shift],
            )
            for side in range(2)
            for shift in range(4)
        ]

    def fetch(plane):
        for core in range(2):

            @pl.when(place[1] == core)
            def _():
                for copy in copies(core, plane):
                    copy.start()

    fetch(0)
    fetch(1)
    out[...] = jnp.zeros_like(out)
    for head in range(16):
        firsts, lasts = [], []
        for position in range(4):
            block = attended[position * 16 + head].astype(F32)
            packed = block[SLOTS : SLOTS + 8]
            firsts.append(block[0:SLOTS])
            lasts.append(packed)
            lasts += [pltpu.roll(packed, 128 - 32 * group, 1) for group in range(1, 4)]
            lasts.append(block[SLOTS + 8 : SLOTS + 16])
        rows[head, :, 0:128] = jnp.concatenate(firsts, axis=0).astype(BF16)
        rows[head, :, 128:256] = jnp.concatenate(lasts, axis=0).astype(BF16)
    def one_plane(plane, carry):
        for copy in copies(0, plane):
            copy.wait()

        @pl.when(plane < 2)
        def _():
            fetch(plane + 2)

        for start, width in ((0, 256), (256, 256), (512, 128)):
            column = pl.multiple_of(640 * plane + start, 128)
            total = jnp.zeros((BLOCK, width), F32)
            for head in range(16):
                partial = jnp.dot(
                    rows[head, :, 0:HD],
                    weights[head // 4, head % 4, :, pl.ds(column, width)],
                    preferred_element_type=F32,
                )
                total += partial.astype(BF16).astype(F32)
            for tile in range(width // 128):
                mixed[5 * plane + start // 128 + tile] = total[:, tile * 128 : (tile + 1) * 128]
        return carry

    lax.fori_loop(0, 4, one_plane, 0)
    for slot in range(SLOTS):
        window = slots[slot]

        @pl.when(window >= 0)
        def _():
            term = jnp.concatenate(
                [mixed[tile, pl.ds(slot, 4, stride=SLOTS), :] for tile in range(TILES)], axis=1
            )
            out[window] = (grid_ref[window].astype(F32) + term).astype(BF16)


def finish(slots, place, windows, attended, mine, other):
    return pl.pallas_call(
        finish_kernel,
        out_shape=jax.ShapeDtypeStruct((WINDOWS, 4, D), BF16),
        in_specs=[SMEM, SMEM, VMEM, VMEM, ANY, ANY],
        out_specs=VMEM,
        scratch_shapes=[
            pltpu.VMEM((4, 4, HD, D), BF16),
            pltpu.VMEM((16, BLOCK, 256), BF16),
            pltpu.VMEM((TILES, BLOCK, 128), F32),
            pltpu.SemaphoreType.DMA((32,)),
        ],
        compiler_params=params(),
        cost_estimate=pl.CostEstimate(
            flops=2 * BLOCK * D * D, bytes_accessed=2 * D * D, transcendentals=0
        ),
        name="finish",
    )(slots, place, windows, attended, mine, other)


def shards(grid, keep_list, ln_gain, ln_bias, w_qkv, w_out):
    z, core, y, x = (lax.axis_index(name) for name in ("z", "c", "y", "x"))
    place = jnp.stack([z, core, y, x]).astype(jnp.int32)
    slots = keep_list[0, 0]
    windows = grid.reshape(WINDOWS, 4, D)

    swap = lambda array: lax.ppermute(array, "c", ring(2, 1))
    piece = quarter_of(place, jnp.swapaxes(w_qkv, 1, 2))
    heads = lax.all_gather(piece, ("z", "x"), axis=0)

    slots_after = lax.optimization_barrier((slots, piece))[0]
    normed = normed_tokens(
        slots_after, place, windows, ln_gain.reshape(TILES, 128), ln_bias.reshape(TILES, 128)
    )
    own = jnp.concatenate(
        [normed[0]] + [lax.ppermute(normed[shift], "z", ring(4, shift)) for shift in (1, 2, 3)],
        axis=0,
    )
    below = lax.ppermute(own, "y", ring(4, 1))
    above = lax.ppermute(own, "y", ring(4, 3))
    far_top = lax.ppermute(below[: BLOCK // 2], "y", ring(4, 1))
    far_bottom = lax.ppermute(above[BLOCK // 2 :], "y", ring(4, 3))

    eighth = lax.dynamic_slice(w_out, (core * 80, z * 640), (80, 640))
    row = jnp.stack([eighth] + [lax.ppermute(eighth, "x", ring(4, shift)) for shift in (1, 2, 3)])
    row = lax.optimization_barrier((row, far_top, far_bottom))[0]
    w_out_mine = lax.all_gather(row, ("z", "y"), axis=0)

    tokens = [own, below, above, far_top, far_bottom]
    tokens = tokens + [swap(part) for part in tokens]
    to_next, to_last = project(place, tokens, heads, (1, 3))
    tokens = lax.optimization_barrier((*tokens, to_next))[:10]
    to_far, to_own = project(place, tokens, heads, (2, 0))
    local = [to_own, lax.ppermute(to_next, "x", ring(4, 1)), lax.ppermute(to_last, "x", ring(4, 3))]
    remote = [swap(part) for part in local]
    from_far = lax.ppermute(to_far, "x", ring(4, 2))
    state = attend(place, local + remote)
    from_far = lax.optimization_barrier((from_far, *state))[0]
    attended = attend(place, local + [from_far] + remote + [swap(from_far)], state)
    w_out_mine = lax.optimization_barrier((w_out_mine, attended))[0]
    w_out_other = swap(w_out_mine)
    attended = lax.all_to_all(attended, ("z", "y", "x"), 0, 0, tiled=True)
    result = finish(slots, place, windows, attended, w_out_mine, w_out_other)
    return result.reshape(grid.shape)


def solution(mesh):
    split = Mesh(mesh.devices.reshape(4, 2, 4, 4), ("z", "c", "y", "x"))
    lat, lon = ("z", "c"), ("y", "x")
    placed = (
        P(lat, lon, None, None),
        P(lat, lon, None),
        P(),
        P(),
        P(lon, None, None),
        P(lon, None),
    )
    return jax.shard_map(
        shards, mesh=split, in_specs=placed, out_specs=P(lat, lon, None, None), check_vma=False
    )
```

```python
import functools
import math

import jax
import jax.numpy as jnp
from jax import lax
from jax.experimental import pallas as pl
from jax.experimental.pallas import tpu as pltpu
from jax.sharding import Mesh
from jax.sharding import PartitionSpec as P

EPSILON = 1e-05
SLOTS = 40
WINDOWS = 64
D = 2560
TILES = D // 128
HD = 160
BLOCK = 4 * SLOTS
COLUMN = 4 * BLOCK
QUERIES = 320
MASKED = -1e30
UNUSED = 1024.0
VMEM_LIMIT = 60 * 1024 * 1024
HALVES = ((0, 32), (64, 96), (160, 192), (224, 256), (320, 352), (384, 416), (128, 288), (448, 0))
BF16 = jnp.bfloat16
F32 = jnp.float32
ANY = pl.BlockSpec(memory_space=pl.ANY)
VMEM = pl.BlockSpec(memory_space=pltpu.VMEM)
SMEM = pl.BlockSpec(memory_space=pltpu.SMEM)


def ring(size, shift):
    return [(i, (i + shift) % size) for i in range(size)]


def params():
    return pltpu.CompilerParams(vmem_limit_bytes=VMEM_LIMIT)


def normed_kernel(slots, place, grid_ref, gain_ref, bias_ref, *refs):
    gain = jnp.concatenate([gain_ref[tile : tile + 1, :] for tile in range(TILES)], axis=1)
    bias = jnp.concatenate([bias_ref[tile : tile + 1, :] for tile in range(TILES)], axis=1)
    outs, tokens = refs[:4], refs[4]
    used = jnp.int32(0)
    for slot in range(SLOTS):
        window = slots[slot]
        used += (window >= 0).astype(jnp.int32)
        loaded = grid_ref[jnp.maximum(window, 0)].astype(F32)
        for tile in range(TILES):
            tokens[tile, pl.ds(4 * slot, 4), :] = loaded[:, tile * 128 : (tile + 1) * 128]
    kept = lax.broadcasted_iota(jnp.int32, (SLOTS, 1), 0) < used
    for shift in range(4):
        position = lax.rem(place[0] + shift, 4)
        values = jnp.concatenate(
            [tokens[tile, pl.ds(position, SLOTS, stride=4), :] for tile in range(TILES)], axis=1
        )
        center = jnp.mean(values, axis=1, keepdims=True)
        moved = values - center
        variance = jnp.mean(moved * moved, axis=1, keepdims=True)
        normed = moved * lax.rsqrt(variance + EPSILON) * gain + bias
        outs[shift][...] = jnp.where(kept, normed, UNUSED).astype(BF16)


def normed_tokens(slots, place, windows, gain, bias):
    return pl.pallas_call(
        normed_kernel,
        out_shape=[jax.ShapeDtypeStruct((SLOTS, D), BF16)] * 4,
        in_specs=[SMEM, SMEM, VMEM, VMEM, VMEM],
        out_specs=[VMEM] * 4,
        scratch_shapes=[pltpu.VMEM((TILES, 4 * SLOTS + 8, 128), F32)],
        compiler_params=params(),
        name="normed",
    )(slots, place, windows, gain, bias)


def piece_kernel(place, raw, piece, sems):
    quarter = 4 * place[1] + place[0]
    for part in range(2):
        first = jnp.int32(HALVES[0][part])
        for i in range(1, 8):
            first = jnp.where(quarter == i, HALVES[i][part], first)
        pltpu.make_async_copy(
            raw.at[0, pl.ds(pl.multiple_of(first, 32), 32)],
            piece.at[pl.ds(32 * part, 32)],
            sems.at[part],
        ).start()
    for part in range(2):
        pltpu.make_async_copy(
            raw.at[0, pl.ds(0, 32)], piece.at[pl.ds(32 * part, 32)], sems.at[part]
        ).wait()


def quarter_of(place, raw):
    return pl.pallas_call(
        piece_kernel,
        out_shape=jax.ShapeDtypeStruct((64, D), BF16),
        in_specs=[SMEM, ANY],
        out_specs=VMEM,
        scratch_shapes=[pltpu.SemaphoreType.DMA((2,))],
        compiler_params=params(),
        name="quarter",
    )(place, raw)


def project_kernel(rows, shifts, place, *refs):
    count, heads = len(rows), len(shifts)
    pieces, weights, refs = refs[:count], refs[count], refs[count + 1 :]
    outs, (tokens, held, token_sems, weight_sems) = refs[:heads], refs[heads:]
    token_copies = []
    total = 0
    for i in range(count):
        token_copies.append(
            pltpu.make_async_copy(pieces[i], tokens.at[pl.ds(total, rows[i])], token_sems.at[i])
        )
        total += rows[i]
    weight_copies = [
        [
            pltpu.make_async_copy(
                weights.at[4 * plane + lax.rem(place[3] + shift, 4)],
                held.at[pl.ds(256 * head + 64 * plane, 64)],
                weight_sems.at[4 * head + plane],
            )
            for plane in range(4)
        ]
        for head, shift in enumerate(shifts)
    ]
    for copy in [copy for made in weight_copies for copy in made] + token_copies:
        copy.start()
    for made in weight_copies:
        for copy in made:
            copy.wait()
    lane = lax.broadcasted_iota(jnp.int32, (COLUMN, 128), 1)
    flagged = (lane >= 96) & (place[1] == 1)
    waited = 0
    for start in range(0, total, COLUMN):
        stop = start + COLUMN
        while waited < count and sum(rows[:waited]) < stop:
            token_copies[waited].wait()
            waited += 1
        chunk = tokens[start:stop]
        mask = jnp.where(chunk[:, 0:128].astype(F32)[:, 0:1] > UNUSED / 2, MASKED, 0.0)
        flags = jnp.where(lane == 96, mask, jnp.where(lane == 97, 1.0, 0.0))
        result = lax.dot_general(
            chunk, held[...], (((1,), (1,)), ((), ())), preferred_element_type=F32
        )
        for head in range(heads):
            base = 256 * head
            outs[head][start:stop, 0:128] = result[:, base : base + 128].astype(BF16)
            outs[head][start:stop, 128:256] = jnp.where(
                flagged, flags, result[:, base + 128 : base + 256]
            ).astype(BF16)


def project(place, pieces, weights, shifts):
    rows = tuple(piece.shape[0] for piece in pieces)
    total, heads = sum(rows), len(shifts)
    return pl.pallas_call(
        functools.partial(project_kernel, rows, shifts),
        out_shape=[jax.ShapeDtypeStruct((total, 256), BF16)] * heads,
        in_specs=[SMEM] + [ANY] * (len(pieces) + 1),
        out_specs=[VMEM] * heads,
        scratch_shapes=[
            pltpu.VMEM((total, D), BF16),
            pltpu.VMEM((heads * 256, D), BF16),
            pltpu.SemaphoreType.DMA((len(pieces),)),
            pltpu.SemaphoreType.DMA((4 * heads,)),
        ],
        compiler_params=params(),
        cost_estimate=pl.CostEstimate(
            flops=2 * total * D * 256 * heads,
            bytes_accessed=total * D * 2 + D * 512 * heads,
            transcendentals=0,
        ),
        name="project",
    )(place, *pieces, weights)


def attend_kernel(first, place, *refs):
    count = 3 if first else 4
    sources, refs = refs[: 2 * count], refs[2 * count :]
    if first:
        sums, tops, held, turned, scores, sems = refs
    else:
        sums, tops, out, held, turned, scores, sems = refs
    near, far = [i for i in range(2 * count) if i % count < 3], [3, 7]
    copies = []
    for i in range(2 * count):
        step, foreign = i % count, i // count
        copies.append([])
        for side in range(2):
            base = pl.multiple_of((1 - place[1] if side else place[1]) * 256, 256)
            copies[i].append(
                pltpu.make_async_copy(
                    sources[count * side + step].at[pl.ds(COLUMN * (foreign ^ side), COLUMN)],
                    held.at[i, :, pl.ds(base, 256)],
                    sems.at[2 * i + side],
                )
            )
    for i in near if first else far + near:
        for copy in copies[i]:
            copy.start()
    lane = lax.broadcasted_iota(jnp.int32, (QUERIES, 128), 1)
    scale = math.log2(math.e) / HD**0.5

    def arrive(piece):
        for copy in copies[piece]:
            copy.wait()

    def turn(piece):
        turned[piece, 0:128, :] = held[piece, :, 128:256].T
        turned[piece, 128:256, :] = held[piece, :, 384:512].T

    def queries_of(index):
        step, half = index // 2, index % 2
        rows = pl.ds(pl.multiple_of(half * QUERIES, QUERIES), QUERIES)
        tail = pltpu.roll(held[step, rows, 384:512].astype(F32), 32, 1)
        tail = jnp.where(
            (lane >= 32) & (lane < 64), tail, jnp.where(lane == 96, 1.0, 0.0)
        ).astype(BF16)
        return jnp.concatenate([held[step, rows, 0:128], tail], axis=1)

    def score(queries, slot, place_, piece, top):
        result = jnp.dot(queries, turned[piece], preferred_element_type=F32)
        scores[slot, :, place_ * COLUMN : (place_ + 1) * COLUMN] = result
        for tile in range(COLUMN // 128):
            part = result[:, tile * 128 : (tile + 1) * 128]
            top = part if top is None else jnp.maximum(top, part)
        return top

    def weigh(slot, place_, piece, peak, total):
        weights = jnp.exp2(
            (scores[slot, :, place_ * COLUMN : (place_ + 1) * COLUMN] - peak) * scale
        ).astype(BF16)
        values = jnp.concatenate([held[piece, :, 256:384], held[piece, :, 384:512]], axis=1)
        result = jnp.dot(weights, values, preferred_element_type=F32)
        return result if total is None else total + result

    def carried(index, peak):
        before = tops[index][:, 0:1]
        joint = jnp.maximum(peak, before)
        return joint, sums[index] * jnp.exp2((before - joint) * scale)

    def keep(index, peak, total):
        sums[index] = total
        tops[index] = jnp.broadcast_to(peak, (QUERIES, 128))

    def emit(index, peak, total):
        step, half = divmod(index, 2)
        x_shift = (0, 1, 3, 2)[step]
        inverse = 1.0 / total[:, 225:226]
        start = total[:, 0:128] * inverse
        last = pltpu.roll(total[:, 128:256] * inverse, 64, 1)
        last = jnp.where(lane < 32, last, 0.0)
        for part in range(8):
            y_shift = half * 3 if part < 4 else 1 + half
            target = (
                lax.rem(place[0] + 4 - part % 4, 4) * 16
                + lax.rem(place[2] + 4 - y_shift, 4) * 4
                + lax.rem(place[3] + 4 - x_shift, 4)
            )
            base = part * SLOTS
            packed = last[base : base + 8]
            for group in range(1, 4):
                rows = last[base + 8 * group : base + 8 * group + 8]
                packed += pltpu.roll(rows, 32 * group, 1)
            out[target] = jnp.concatenate(
                [start[base : base + SLOTS], packed, last[base + 32 : base + SLOTS]], axis=0
            ).astype(BF16)

    def alone(index, peak):
        return peak, None

    if first:
        blocks = [(index, near, alone, keep) for index in range(6)]
        turns = {}
    else:
        blocks = [(index, far, carried, emit) for index in range(6)]
        blocks += [(index, near + far, alone, emit) for index in (6, 7)]
        turns = {0: near[:2], 1: near[2:3], 2: near[3:4], 3: near[4:5], 4: near[5:]}
        for piece in far + near:
            arrive(piece)
        for piece in far:
            turn(piece)
    top, queries = None, None
    for i, piece in enumerate(blocks[0][1]):
        if first:
            arrive(piece)
            turn(piece)
        queries = queries_of(0) if queries is None else queries
        top = score(queries, 0, i, piece, top)
    if first:

        def two_blocks(pair, peak):
            for slot in range(2):
                index = 2 * pair + slot
                queries, top, total = queries_of(jnp.minimum(index + 1, 5)), None, None
                for i, piece in enumerate(near):
                    top = score(queries, 1 - slot, i, piece, top)
                    total = weigh(slot, i, piece, peak, total)
                keep(index, peak, total)
                peak = jnp.max(top, axis=1, keepdims=True)
            return peak

        lax.fori_loop(0, 3, two_blocks, jnp.max(top, axis=1, keepdims=True))
        return
    for number, (index, pieces, begin, end) in enumerate(blocks):
        peak, total = begin(index, jnp.max(top, axis=1, keepdims=True))
        for piece in turns.get(number, ()):
            turn(piece)
        ahead = ()
        if number + 1 < len(blocks):
            ahead, queries, top = blocks[number + 1][1], queries_of(blocks[number + 1][0]), None
        for i in range(max(len(pieces), len(ahead))):
            if i < len(ahead):
                top = score(queries, (number + 1) % 2, i, ahead[i], top)
            if i < len(pieces):
                total = weigh(number % 2, i, pieces[i], peak, total)
        end(index, peak, total)


def attend(place, sources, state=None):
    first = state is None
    pieces = len(sources)
    sums = jax.ShapeDtypeStruct((6, QUERIES, 256), F32)
    tops = jax.ShapeDtypeStruct((6, QUERIES, 128), F32)
    whole = jax.ShapeDtypeStruct((64, SLOTS + 16, 128), BF16)
    work = 9 if first else 7
    return pl.pallas_call(
        functools.partial(attend_kernel, first),
        out_shape=[sums, tops] if first else whole,
        in_specs=[SMEM] + [ANY] * pieces + ([] if first else [VMEM, VMEM]),
        out_specs=[VMEM, VMEM] if first else VMEM,
        scratch_shapes=[
            pltpu.VMEM((pieces, COLUMN, 512), BF16),
            pltpu.VMEM((pieces, 256, COLUMN), BF16),
            pltpu.VMEM((2, QUERIES, pieces * COLUMN), F32),
            pltpu.SemaphoreType.DMA((2 * pieces,)),
        ],
        compiler_params=params(),
        cost_estimate=pl.CostEstimate(
            flops=2 * COLUMN * COLUMN * 4 * 256 * work,
            bytes_accessed=pieces * COLUMN * 1024,
            transcendentals=2 * COLUMN * COLUMN * work,
        ),
        name="attend",
    )(place, *sources, *(state or ()))


def finish_kernel(slots, place, grid_ref, attended, mine, other, out, weights, rows, mixed, sems):
    def copies(core, plane):
        return [
            pltpu.make_async_copy(
                (mine, other)[side].at[pl.ds(4 * plane, 4), shift],
                weights.at[
                    :,
                    lax.rem(place[3] + 4 - shift, 4),
                    pl.ds(80 * (side ^ core), 80),
                    pl.ds(pl.multiple_of(640 * plane, 128), 640),
                ],
                sems.at[8 * plane + 4 * side + shift],
            )
            for side in range(2)
            for shift in range(4)
        ]

    def fetch(plane):
        for core in range(2):

            @pl.when(place[1] == core)
            def _():
                for copy in copies(core, plane):
                    copy.start()

    fetch(0)
    fetch(1)
    out[...] = jnp.zeros_like(out)
    for head in range(16):
        firsts, lasts = [], []
        for position in range(4):
            block = attended[position * 16 + head].astype(F32)
            packed = block[SLOTS : SLOTS + 8]
            firsts.append(block[0:SLOTS])
            lasts.append(packed)
            lasts += [pltpu.roll(packed, 128 - 32 * group, 1) for group in range(1, 4)]
            lasts.append(block[SLOTS + 8 : SLOTS + 16])
        rows[head, :, 0:128] = jnp.concatenate(firsts, axis=0).astype(BF16)
        rows[head, :, 128:256] = jnp.concatenate(lasts, axis=0).astype(BF16)
    def one_plane(plane, carry):
        for copy in copies(0, plane):
            copy.wait()

        @pl.when(plane < 2)
        def _():
            fetch(plane + 2)

        for start, width in ((0, 256), (256, 256), (512, 128)):
            column = pl.multiple_of(640 * plane + start, 128)
            total = jnp.zeros((BLOCK, width), F32)
            for head in range(16):
                partial = jnp.dot(
                    rows[head, :, 0:HD],
                    weights[head // 4, head % 4, :, pl.ds(column, width)],
                    preferred_element_type=F32,
                )
                total += partial.astype(BF16).astype(F32)
            for tile in range(width // 128):
                mixed[5 * plane + start // 128 + tile, 0:BLOCK, :] = total[
                    :, tile * 128 : (tile + 1) * 128
                ]
        return carry

    lax.fori_loop(0, 4, one_plane, 0)
    for slot in range(SLOTS):
        window = slots[slot]

        @pl.when(window >= 0)
        def _():
            term = jnp.concatenate(
                [mixed[tile, pl.ds(slot, 4, stride=SLOTS), :] for tile in range(TILES)], axis=1
            )
            out[window] = (grid_ref[window].astype(F32) + term).astype(BF16)


def finish(slots, place, windows, attended, mine, other):
    return pl.pallas_call(
        finish_kernel,
        out_shape=jax.ShapeDtypeStruct((WINDOWS, 4, D), BF16),
        in_specs=[SMEM, SMEM, VMEM, VMEM, ANY, ANY],
        out_specs=VMEM,
        scratch_shapes=[
            pltpu.VMEM((4, 4, HD, D), BF16),
            pltpu.VMEM((16, BLOCK, 256), BF16),
            pltpu.VMEM((TILES, BLOCK + SLOTS, 128), F32),
            pltpu.SemaphoreType.DMA((32,)),
        ],
        compiler_params=params(),
        cost_estimate=pl.CostEstimate(
            flops=2 * BLOCK * D * D, bytes_accessed=2 * D * D, transcendentals=0
        ),
        name="finish",
    )(slots, place, windows, attended, mine, other)


def shards(grid, keep_list, ln_gain, ln_bias, w_qkv, w_out):
    z, core, y, x = (lax.axis_index(name) for name in ("z", "c", "y", "x"))
    place = jnp.stack([z, core, y, x]).astype(jnp.int32)
    slots = keep_list[0, 0]
    windows = grid.reshape(WINDOWS, 4, D)

    swap = lambda array: lax.ppermute(array, "c", ring(2, 1))
    piece = quarter_of(place, jnp.swapaxes(w_qkv, 1, 2))
    heads = lax.all_gather(piece, ("z", "x"), axis=0)

    slots_after = lax.optimization_barrier((slots, piece))[0]
    normed = normed_tokens(
        slots_after, place, windows, ln_gain.reshape(TILES, 128), ln_bias.reshape(TILES, 128)
    )
    own = jnp.concatenate(
        [normed[0]] + [lax.ppermute(normed[shift], "z", ring(4, shift)) for shift in (1, 2, 3)],
        axis=0,
    )
    below = lax.ppermute(own, "y", ring(4, 1))
    above = lax.ppermute(own, "y", ring(4, 3))
    far_top = lax.ppermute(below[: BLOCK // 2], "y", ring(4, 1))
    far_bottom = lax.ppermute(above[BLOCK // 2 :], "y", ring(4, 3))

    eighth = lax.dynamic_slice(w_out, (core * 80, z * 640), (80, 640))
    row = jnp.stack([eighth] + [lax.ppermute(eighth, "x", ring(4, shift)) for shift in (1, 2, 3)])
    row = lax.optimization_barrier((row, far_top, far_bottom))[0]
    w_out_mine = lax.all_gather(row, ("z", "y"), axis=0)

    tokens = [own, below, above, far_top, far_bottom]
    tokens = tokens + [swap(part) for part in tokens]
    to_next, to_last = project(place, tokens, heads, (1, 3))
    tokens = lax.optimization_barrier((*tokens, to_next))[:10]
    to_far, to_own = project(place, tokens, heads, (2, 0))
    local = [to_own, lax.ppermute(to_next, "x", ring(4, 1)), lax.ppermute(to_last, "x", ring(4, 3))]
    remote = [swap(part) for part in local]
    from_far = lax.ppermute(to_far, "x", ring(4, 2))
    state = attend(place, local + remote)
    from_far = lax.optimization_barrier((from_far, *state))[0]
    attended = attend(place, local + [from_far] + remote + [swap(from_far)], state)
    w_out_mine = lax.optimization_barrier((w_out_mine, attended))[0]
    w_out_other = swap(w_out_mine)
    attended = lax.all_to_all(attended, ("z", "y", "x"), 0, 0, tiled=True)
    result = finish(slots, place, windows, attended, w_out_mine, w_out_other)
    return result.reshape(grid.shape)


def solution(mesh):
    split = Mesh(mesh.devices.reshape(4, 2, 4, 4), ("z", "c", "y", "x"))
    lat, lon = ("z", "c"), ("y", "x")
    placed = (
        P(lat, lon, None, None),
        P(lat, lon, None),
        P(),
        P(),
        P(lon, None, None),
        P(lon, None),
    )
    return jax.shard_map(
        shards, mesh=split, in_specs=placed, out_specs=P(lat, lon, None, None), check_vma=False
    )
```

```python
import functools
import math

import jax
import jax.numpy as jnp
from jax import lax
from jax.experimental import pallas as pl
from jax.experimental.pallas import tpu as pltpu
from jax.sharding import Mesh
from jax.sharding import PartitionSpec as P

EPSILON = 1e-05
SLOTS = 40
WINDOWS = 64
D = 2560
TILES = D // 128
HD = 160
BLOCK = 4 * SLOTS
COLUMN = 4 * BLOCK
QUERIES = 320
MASKED = -1e30
UNUSED = 1024.0
VMEM_LIMIT = 60 * 1024 * 1024
HALVES = ((0, 32), (64, 96), (160, 192), (224, 256), (320, 352), (384, 416), (128, 288), (448, 0))
BF16 = jnp.bfloat16
F32 = jnp.float32
ANY = pl.BlockSpec(memory_space=pl.ANY)
VMEM = pl.BlockSpec(memory_space=pltpu.VMEM)
SMEM = pl.BlockSpec(memory_space=pltpu.SMEM)


def ring(size, shift):
    return [(i, (i + shift) % size) for i in range(size)]


def params():
    return pltpu.CompilerParams(vmem_limit_bytes=VMEM_LIMIT)


def normed_kernel(slots, place, grid_ref, gain_ref, bias_ref, *refs):
    gain = jnp.concatenate([gain_ref[tile : tile + 1, :] for tile in range(TILES)], axis=1)
    bias = jnp.concatenate([bias_ref[tile : tile + 1, :] for tile in range(TILES)], axis=1)
    outs, tokens = refs[:4], refs[4]
    used = jnp.int32(0)
    for slot in range(SLOTS):
        window = slots[slot]
        used += (window >= 0).astype(jnp.int32)
        loaded = grid_ref[jnp.maximum(window, 0)].astype(F32)
        for tile in range(TILES):
            tokens[tile, pl.ds(4 * slot, 4), :] = loaded[:, tile * 128 : (tile + 1) * 128]
    kept = lax.broadcasted_iota(jnp.int32, (SLOTS, 1), 0) < used
    for shift in range(4):
        position = lax.rem(place[0] + shift, 4)
        values = jnp.concatenate(
            [tokens[tile, pl.ds(position, SLOTS, stride=4), :] for tile in range(TILES)], axis=1
        )
        center = jnp.mean(values, axis=1, keepdims=True)
        moved = values - center
        variance = jnp.mean(moved * moved, axis=1, keepdims=True)
        normed = moved * lax.rsqrt(variance + EPSILON) * gain + bias
        outs[shift][...] = jnp.where(kept, normed, UNUSED).astype(BF16)


def normed_tokens(slots, place, windows, gain, bias):
    return pl.pallas_call(
        normed_kernel,
        out_shape=[jax.ShapeDtypeStruct((SLOTS, D), BF16)] * 4,
        in_specs=[SMEM, SMEM, VMEM, VMEM, VMEM],
        out_specs=[VMEM] * 4,
        scratch_shapes=[pltpu.VMEM((TILES, 4 * SLOTS + 8, 128), F32)],
        compiler_params=params(),
        name="normed",
    )(slots, place, windows, gain, bias)


def piece_kernel(place, raw, piece, sems):
    quarter = 4 * place[1] + place[0]
    for part in range(2):
        first = jnp.int32(HALVES[0][part])
        for i in range(1, 8):
            first = jnp.where(quarter == i, HALVES[i][part], first)
        pltpu.make_async_copy(
            raw.at[0, pl.ds(pl.multiple_of(first, 32), 32)],
            piece.at[pl.ds(32 * part, 32)],
            sems.at[part],
        ).start()
    for part in range(2):
        pltpu.make_async_copy(
            raw.at[0, pl.ds(0, 32)], piece.at[pl.ds(32 * part, 32)], sems.at[part]
        ).wait()


def quarter_of(place, raw):
    return pl.pallas_call(
        piece_kernel,
        out_shape=jax.ShapeDtypeStruct((64, D), BF16),
        in_specs=[SMEM, ANY],
        out_specs=VMEM,
        scratch_shapes=[pltpu.SemaphoreType.DMA((2,))],
        compiler_params=params(),
        name="quarter",
    )(place, raw)


def project_kernel(rows, shifts, place, *refs):
    count, heads = len(rows), len(shifts)
    pieces, weights, refs = refs[:count], refs[count], refs[count + 1 :]
    outs, (tokens, held, token_sems, weight_sems) = refs[:heads], refs[heads:]
    token_copies = []
    total = 0
    for i in range(count):
        token_copies.append(
            pltpu.make_async_copy(pieces[i], tokens.at[pl.ds(total, rows[i])], token_sems.at[i])
        )
        total += rows[i]
    weight_copies = [
        [
            pltpu.make_async_copy(
                weights.at[4 * plane + lax.rem(place[3] + shift, 4)],
                held.at[pl.ds(256 * head + 64 * plane, 64)],
                weight_sems.at[4 * head + plane],
            )
            for plane in range(4)
        ]
        for head, shift in enumerate(shifts)
    ]
    for copy in [copy for made in weight_copies for copy in made] + token_copies:
        copy.start()
    for made in weight_copies:
        for copy in made:
            copy.wait()
    lane = lax.broadcasted_iota(jnp.int32, (COLUMN, 128), 1)
    flagged = (lane >= 96) & (place[1] == 1)
    waited = 0
    for start in range(0, total, COLUMN):
        stop = start + COLUMN
        while waited < count and sum(rows[:waited]) < stop:
            token_copies[waited].wait()
            waited += 1
        chunk = tokens[start:stop]
        mask = jnp.where(chunk[:, 0:128].astype(F32)[:, 0:1] > UNUSED / 2, MASKED, 0.0)
        flags = jnp.where(lane == 96, mask, jnp.where(lane == 97, 1.0, 0.0))
        result = lax.dot_general(
            chunk, held[...], (((1,), (1,)), ((), ())), preferred_element_type=F32
        )
        for head in range(heads):
            base = 256 * head
            outs[head][start:stop, 0:128] = result[:, base : base + 128].astype(BF16)
            outs[head][start:stop, 128:256] = jnp.where(
                flagged, flags, result[:, base + 128 : base + 256]
            ).astype(BF16)


def project(place, pieces, weights, shifts):
    rows = tuple(piece.shape[0] for piece in pieces)
    total, heads = sum(rows), len(shifts)
    return pl.pallas_call(
        functools.partial(project_kernel, rows, shifts),
        out_shape=[jax.ShapeDtypeStruct((total, 256), BF16)] * heads,
        in_specs=[SMEM] + [ANY] * (len(pieces) + 1),
        out_specs=[VMEM] * heads,
        scratch_shapes=[
            pltpu.VMEM((total, D), BF16),
            pltpu.VMEM((heads * 256, D), BF16),
            pltpu.SemaphoreType.DMA((len(pieces),)),
            pltpu.SemaphoreType.DMA((4 * heads,)),
        ],
        compiler_params=params(),
        cost_estimate=pl.CostEstimate(
            flops=2 * total * D * 256 * heads,
            bytes_accessed=total * D * 2 + D * 512 * heads,
            transcendentals=0,
        ),
        name="project",
    )(place, *pieces, weights)


def attend_kernel(first, place, *refs):
    count = 3 if first else 4
    sources, refs = refs[: 2 * count], refs[2 * count :]
    if first:
        sums, tops, held, turned, scores, sems = refs
    else:
        sums, tops, out, held, turned, scores, sems = refs
    near, far = [i for i in range(2 * count) if i % count < 3], [3, 7]
    copies = []
    for i in range(2 * count):
        step, foreign = i % count, i // count
        copies.append([])
        for side in range(2):
            base = pl.multiple_of((1 - place[1] if side else place[1]) * 256, 256)
            copies[i].append(
                pltpu.make_async_copy(
                    sources[count * side + step].at[pl.ds(COLUMN * (foreign ^ side), COLUMN)],
                    held.at[i, :, pl.ds(base, 256)],
                    sems.at[2 * i + side],
                )
            )
    for i in near if first else far + near:
        for copy in copies[i]:
            copy.start()
    lane = lax.broadcasted_iota(jnp.int32, (QUERIES, 128), 1)
    scale = math.log2(math.e) / HD**0.5

    def arrive(piece):
        for copy in copies[piece]:
            copy.wait()

    def turn(piece):
        turned[piece, 0:128, :] = held[piece, :, 128:256].T
        turned[piece, 128:256, :] = held[piece, :, 384:512].T

    def queries_of(index):
        step, half = index // 2, index % 2
        rows = pl.ds(pl.multiple_of(half * QUERIES, QUERIES), QUERIES)
        tail = pltpu.roll(held[step, rows, 384:512].astype(F32), 32, 1)
        tail = jnp.where(
            (lane >= 32) & (lane < 64), tail, jnp.where(lane == 96, 1.0, 0.0)
        ).astype(BF16)
        return jnp.concatenate([held[step, rows, 0:128], tail], axis=1)

    def score(queries, slot, place_, piece, top):
        result = jnp.dot(queries, turned[piece], preferred_element_type=F32)
        scores[slot, :, place_ * COLUMN : (place_ + 1) * COLUMN] = result
        for tile in range(COLUMN // 128):
            part = result[:, tile * 128 : (tile + 1) * 128]
            top = part if top is None else jnp.maximum(top, part)
        return top

    def weigh(slot, place_, piece, peak, total):
        weights = jnp.exp2(
            (scores[slot, :, place_ * COLUMN : (place_ + 1) * COLUMN] - peak) * scale
        ).astype(BF16)
        values = jnp.concatenate([held[piece, :, 256:384], held[piece, :, 384:512]], axis=1)
        result = jnp.dot(weights, values, preferred_element_type=F32)
        return result if total is None else total + result

    def carried(index, peak):
        before = tops[index][:, 0:1]
        joint = jnp.maximum(peak, before)
        return joint, sums[index] * jnp.exp2((before - joint) * scale)

    def keep(index, peak, total):
        sums[index] = total
        tops[index] = jnp.broadcast_to(peak, (QUERIES, 128))

    def emit(index, peak, total):
        step, half = divmod(index, 2)
        x_shift = (0, 1, 3, 2)[step]
        inverse = 1.0 / total[:, 225:226]
        start = total[:, 0:128] * inverse
        last = pltpu.roll(total[:, 128:256] * inverse, 64, 1)
        last = jnp.where(lane < 32, last, 0.0)
        for part in range(8):
            y_shift = half * 3 if part < 4 else 1 + half
            target = (
                lax.rem(place[0] + 4 - part % 4, 4) * 16
                + lax.rem(place[2] + 4 - y_shift, 4) * 4
                + lax.rem(place[3] + 4 - x_shift, 4)
            )
            base = part * SLOTS
            packed = last[base : base + 8]
            for group in range(1, 4):
                rows = last[base + 8 * group : base + 8 * group + 8]
                packed += pltpu.roll(rows, 32 * group, 1)
            out[target] = jnp.concatenate(
                [start[base : base + SLOTS], packed, last[base + 32 : base + SLOTS]], axis=0
            ).astype(BF16)

    def alone(index, peak):
        return peak, None

    if first:
        blocks = [(index, near, alone, keep) for index in range(6)]
        turns = {}
    else:
        blocks = [(index, far, carried, emit) for index in range(6)]
        blocks += [(index, near + far, alone, emit) for index in (6, 7)]
        turns = {0: near[:2], 1: near[2:3], 2: near[3:4], 3: near[4:5], 4: near[5:]}
        for piece in far + near:
            arrive(piece)
        for piece in far:
            turn(piece)
    top, queries = None, None
    for i, piece in enumerate(blocks[0][1]):
        if first:
            arrive(piece)
            turn(piece)
        queries = queries_of(0) if queries is None else queries
        top = score(queries, 0, i, piece, top)
    if first:

        def two_blocks(pair, peak):
            for slot in range(2):
                index = 2 * pair + slot
                queries, top, total = queries_of(jnp.minimum(index + 1, 5)), None, None
                for i, piece in enumerate(near):
                    top = score(queries, 1 - slot, i, piece, top)
                    total = weigh(slot, i, piece, peak, total)
                keep(index, peak, total)
                peak = jnp.max(top, axis=1, keepdims=True)
            return peak

        lax.fori_loop(0, 3, two_blocks, jnp.max(top, axis=1, keepdims=True))
        return
    for number, (index, pieces, begin, end) in enumerate(blocks):
        peak, total = begin(index, jnp.max(top, axis=1, keepdims=True))
        for piece in turns.get(number, ()):
            turn(piece)
        ahead = ()
        if number + 1 < len(blocks):
            ahead, queries, top = blocks[number + 1][1], queries_of(blocks[number + 1][0]), None
        for i in range(max(len(pieces), len(ahead))):
            if i < len(ahead):
                top = score(queries, (number + 1) % 2, i, ahead[i], top)
            if i < len(pieces):
                total = weigh(number % 2, i, pieces[i], peak, total)
        end(index, peak, total)


def attend(place, sources, state=None):
    first = state is None
    pieces = len(sources)
    sums = jax.ShapeDtypeStruct((6, QUERIES, 256), F32)
    tops = jax.ShapeDtypeStruct((6, QUERIES, 128), F32)
    whole = jax.ShapeDtypeStruct((64, SLOTS + 16, 128), BF16)
    work = 9 if first else 7
    return pl.pallas_call(
        functools.partial(attend_kernel, first),
        out_shape=[sums, tops] if first else whole,
        in_specs=[SMEM] + [ANY] * pieces + ([] if first else [VMEM, VMEM]),
        out_specs=[VMEM, VMEM] if first else VMEM,
        scratch_shapes=[
            pltpu.VMEM((pieces, COLUMN, 512), BF16),
            pltpu.VMEM((pieces, 256, COLUMN), BF16),
            pltpu.VMEM((2, QUERIES, pieces * COLUMN), F32),
            pltpu.SemaphoreType.DMA((2 * pieces,)),
        ],
        compiler_params=params(),
        cost_estimate=pl.CostEstimate(
            flops=2 * COLUMN * COLUMN * 4 * 256 * work,
            bytes_accessed=pieces * COLUMN * 1024,
            transcendentals=2 * COLUMN * COLUMN * work,
        ),
        name="attend",
    )(place, *sources, *(state or ()))


def finish_kernel(slots, place, grid_ref, attended, mine, other, out, weights, rows, mixed, sems):
    def copies(core, plane):
        return [
            pltpu.make_async_copy(
                (mine, other)[side].at[pl.ds(4 * plane, 4), shift],
                weights.at[
                    :,
                    lax.rem(place[3] + 4 - shift, 4),
                    pl.ds(80 * (side ^ core), 80),
                    pl.ds(pl.multiple_of(640 * plane, 128), 640),
                ],
                sems.at[8 * plane + 4 * side + shift],
            )
            for side in range(2)
            for shift in range(4)
        ]

    def fetch(plane):
        for core in range(2):

            @pl.when(place[1] == core)
            def _():
                for copy in copies(core, plane):
                    copy.start()

    fetch(0)
    fetch(1)
    out[...] = jnp.zeros_like(out)
    for head in range(16):
        firsts, lasts = [], []
        for position in range(4):
            block = attended[position * 16 + head].astype(F32)
            packed = block[SLOTS : SLOTS + 8]
            firsts.append(block[0:SLOTS])
            lasts.append(packed)
            lasts += [pltpu.roll(packed, 128 - 32 * group, 1) for group in range(1, 4)]
            lasts.append(block[SLOTS + 8 : SLOTS + 16])
        rows[head, :, 0:128] = jnp.concatenate(firsts, axis=0).astype(BF16)
        rows[head, :, 128:256] = jnp.concatenate(lasts, axis=0).astype(BF16)
    def one_plane(plane, carry):
        for copy in copies(0, plane):
            copy.wait()

        @pl.when(plane < 2)
        def _():
            fetch(plane + 2)

        for start, width in ((0, 256), (256, 256), (512, 128)):
            column = pl.multiple_of(640 * plane + start, 128)
            total = jnp.zeros((BLOCK, width), F32)
            for head in range(16):
                partial = jnp.dot(
                    rows[head, :, 0:HD],
                    weights[head // 4, head % 4, :, pl.ds(column, width)],
                    preferred_element_type=F32,
                )
                total += partial.astype(BF16).astype(F32)
            for tile in range(width // 128):
                mixed[5 * plane + start // 128 + tile, 0:BLOCK, :] = total[
                    :, tile * 128 : (tile + 1) * 128
                ]
        return carry

    lax.fori_loop(0, 4, one_plane, 0)
    for slot in range(SLOTS):
        window = slots[slot]

        @pl.when(window >= 0)
        def _():
            term = jnp.concatenate(
                [mixed[tile, pl.ds(slot, 4, stride=SLOTS), :] for tile in range(TILES)], axis=1
            )
            out[window] = (grid_ref[window].astype(F32) + term).astype(BF16)


def finish(slots, place, windows, attended, mine, other):
    return pl.pallas_call(
        finish_kernel,
        out_shape=jax.ShapeDtypeStruct((WINDOWS, 4, D), BF16),
        in_specs=[SMEM, SMEM, VMEM, VMEM, ANY, ANY],
        out_specs=VMEM,
        scratch_shapes=[
            pltpu.VMEM((4, 4, HD, D), BF16),
            pltpu.VMEM((16, BLOCK, 256), BF16),
            pltpu.VMEM((TILES, BLOCK + SLOTS, 128), F32),
            pltpu.SemaphoreType.DMA((32,)),
        ],
        compiler_params=params(),
        cost_estimate=pl.CostEstimate(
            flops=2 * BLOCK * D * D, bytes_accessed=2 * D * D, transcendentals=0
        ),
        name="finish",
    )(slots, place, windows, attended, mine, other)


def shards(grid, keep_list, ln_gain, ln_bias, w_qkv, w_out):
    z, core, y, x = (lax.axis_index(name) for name in ("z", "c", "y", "x"))
    place = jnp.stack([z, core, y, x]).astype(jnp.int32)
    slots = keep_list[0, 0]
    windows = grid.reshape(WINDOWS, 4, D)

    swap = lambda array: lax.ppermute(array, "c", ring(2, 1))
    piece = quarter_of(place, jnp.swapaxes(w_qkv, 1, 2))
    heads = lax.all_gather(piece, ("z", "x"), axis=0)

    slots_after = lax.optimization_barrier((slots, piece))[0]
    normed = normed_tokens(
        slots_after, place, windows, ln_gain.reshape(TILES, 128), ln_bias.reshape(TILES, 128)
    )
    own = jnp.concatenate(
        [normed[0]] + [lax.ppermute(normed[shift], "z", ring(4, shift)) for shift in (1, 2, 3)],
        axis=0,
    )
    eighth = lax.dynamic_slice(w_out, (core * 80, z * 640), (80, 640))
    eighth = lax.optimization_barrier((eighth, own))[0]
    row = jnp.stack([eighth] + [lax.ppermute(eighth, "x", ring(4, shift)) for shift in (1, 2, 3)])
    below = lax.ppermute(own, "y", ring(4, 1))
    above = lax.ppermute(own, "y", ring(4, 3))
    below, above, row = lax.optimization_barrier((below, above, row))
    far_top = lax.ppermute(below[: BLOCK // 2], "y", ring(4, 1))
    far_bottom = lax.ppermute(above[BLOCK // 2 :], "y", ring(4, 3))

    row = lax.optimization_barrier((row, far_top, far_bottom))[0]
    w_out_mine = lax.all_gather(row, ("z", "y"), axis=0)

    tokens = [own, below, above, far_top, far_bottom]
    tokens = tokens + [swap(part) for part in tokens]
    to_next, to_last = project(place, tokens, heads, (1, 3))
    tokens = lax.optimization_barrier((*tokens, to_next))[:10]
    to_far, to_own = project(place, tokens, heads, (2, 0))
    local = [to_own, lax.ppermute(to_next, "x", ring(4, 1)), lax.ppermute(to_last, "x", ring(4, 3))]
    remote = [swap(part) for part in local]
    from_far = lax.ppermute(to_far, "x", ring(4, 2))
    state = attend(place, local + remote)
    from_far = lax.optimization_barrier((from_far, *state))[0]
    attended = attend(place, local + [from_far] + remote + [swap(from_far)], state)
    w_out_mine = lax.optimization_barrier((w_out_mine, attended))[0]
    w_out_other = swap(w_out_mine)
    attended = lax.all_to_all(attended, ("z", "y", "x"), 0, 0, tiled=True)
    result = finish(slots, place, windows, attended, w_out_mine, w_out_other)
    return result.reshape(grid.shape)


def solution(mesh):
    split = Mesh(mesh.devices.reshape(4, 2, 4, 4), ("z", "c", "y", "x"))
    lat, lon = ("z", "c"), ("y", "x")
    placed = (
        P(lat, lon, None, None),
        P(lat, lon, None),
        P(),
        P(),
        P(lon, None, None),
        P(lon, None),
    )
    return jax.shard_map(
        shards, mesh=split, in_specs=placed, out_specs=P(lat, lon, None, None), check_vma=False
    )
```
